32 devices in a mesh: groups: 2 (over y), dom: 4 (over z), segment: 2 (over x), chan: 2 (over core).
Axes of the slice: x: 2, y: 2, z: 4, core: 2. Of those that a mesh axis runs over, the one named last changes fastest.
Arguments:
- latents: bfloat16 [2, 4096, 256], P(None, ('groups', 'dom')), parts along dimension 1, may hold values from -6 to 6
- neighbors: int32 [6, 4096], P(None, ('groups', 'dom')), parts along dimension 1, may hold values from 0 to 511
- edge_coef: float32 [6, 4096], P(None, ('groups', 'dom')), parts along dimension 1, may hold values from 0.25 to 4
- cross_src: int32 [2, 2, 1024], P(None, None, ('groups', 'dom')), parts along dimension 2, may hold values from 0 to 511
- cross_coef: float32 [2, 2, 1024], P(None, None, ('groups', 'dom')), parts along dimension 2, may hold values from 0.25 to 10
- recv_node: int32 [2, 1024], P(None, ('groups', 'dom')), parts along dimension 1, may hold values from 0 to 511
- w_edge: bfloat16 [4, 256, 256], P('segment'), may hold values from -0.375 to 0.375
- w_node_in: bfloat16 [4, 512, 256], P('segment', None, 'chan'), may hold values from -0.044194174 to 0.044194174
- w_node_out: bfloat16 [4, 256, 256], P('segment', 'chan'), may hold values from -0.0625 to 0.0625
- edge_bias: bfloat16 [4, 256], P('segment'), may hold values from -3 to 3
- edge_gain: bfloat16 [4, 256], P('segment'), may hold values from -6 to 6
- node_bias: bfloat16 [4, 256], P('segment', 'chan'), may hold values from -3 to 3
- norm_gain: bfloat16 [4, 256], P('segment'), may hold values from 0.099609375 to 1.8984375
- norm_bias: bfloat16 [4, 256], P('segment'), may hold values from -3 to 3
Outputs:
- outputs: bfloat16 [2, 4096, 256], P('segment', ('groups', 'dom')), parts along dimension 1
The draws below stay inside these ranges and needn't reach their ends.
There are 2 independent parts, one for each index of `groups`. The reference program is written for one: setup_inputs(seed, part) draws one part's arguments, and reference() takes and returns one part's arrays. A program takes and returns all parts, laid end to end along the dimension named above; an argument that names none is the same for every part. Nothing has to cross between parts.
Inputs may be any that keep to these rules, and one draw needn't show every extreme that they name: `neighbors`: rows of the node's own partition.
All inputs are finite; a program needn't handle non-finite values.
Results may differ from the reference program's by a relative error of at most 0.024.
Values may be sent and summed in bfloat16 or wider, within the bound.
No kernel may reach another device: no remote copies, remote signals or barrier semaphores. Data moves between devices by JAX's collectives and lax.ppermute only.
A program may use at most 64 MiB of HBM per device.

```python
import math
import jax
import jax.numpy as jnp
import numpy as np
from jax import lax

D = 256
NODE_DEV = 512
DEG = 6
XDEG = 2
ROUNDS = 2
IFC = 128
NODES = 2048
SLOTS = 512
LAYERS = 4
MICRO = 2
N_CHAN = 2


def walsh_signs(row_ids, col_ids, order):
    bit_count = order.bit_length() - 1
    parity = jnp.zeros((row_ids.shape[0], col_ids.shape[0]), jnp.int32)
    for place in range(bit_count):
        step = 2 ** place
        row_bit = row_ids // step % 2
        col_bit = col_ids // step % 2
        parity = parity + row_bit[:, None] * col_bit[None, :]
    return (1 - 2 * (parity % 2)).astype(jnp.float32)


def signed_block(key, order, columns):
    keys = jax.random.split(key, 4)
    row_perm = jax.random.permutation(keys[0], order).astype(jnp.int32)
    col_perm = jax.random.permutation(keys[1], order).astype(jnp.int32)[:columns]
    row_flip = (2 * jax.random.randint(keys[2], (order,), 0, 2) - 1).astype(jnp.float32)
    col_flip = (2 * jax.random.randint(keys[3], (columns,), 0, 2) - 1).astype(jnp.float32)
    table = walsh_signs(row_perm, col_perm, order)
    return table * row_flip[:, None] * col_flip[None, :] * float(order) ** (-0.5)


def draw_w_node_in(key, part):
    key = jax.random.fold_in(key, 11)
    layer_keys = jax.random.split(key, LAYERS)
    blocks = [signed_block(layer_keys[layer], 2 * D, D) for layer in range(LAYERS)]
    return jnp.stack(blocks, axis=0).astype(jnp.bfloat16)


def draw_w_node_out(key, part):
    key = jax.random.fold_in(key, 23)
    layer_keys = jax.random.split(key, LAYERS)
    blocks = [signed_block(layer_keys[layer], D, D) for layer in range(LAYERS)]
    return jnp.stack(blocks, axis=0).astype(jnp.bfloat16)


def touch_ends(entries, own_key, low, high):
    spot = [jax.random.randint(jax.random.fold_in(own_key, axis), (), 0, length) for axis, length in enumerate(entries.shape)]
    widest = entries.shape.index(max(entries.shape))
    next_to = spot[:widest] + [(spot[widest] + 1) % entries.shape[widest]] + spot[widest + 1:]
    return entries.at[tuple(spot)].set(low).at[tuple(next_to)].set(high)


def levels(own_key, extent, pieces, low, top_value):
    loudness, own = 1.0, jax.random.fold_in(own_key, 6)
    for position, shards_of in pieces:
        draws = jnp.exp(jax.random.uniform(jax.random.fold_in(own, position), (shards_of,), jnp.float32, low / len(pieces), top_value / len(pieces)))
        loudness = loudness * jnp.repeat(draws, extent[position] // shards_of).reshape([-1 if axis == position else 1 for axis in range(len(extent))])
    return loudness


def noise(key, shape, deviation, limit, pieces=(), kind=jnp.bfloat16):
    array = deviation * jax.random.normal(key, shape, jnp.float32)
    if pieces:
        array = array * levels(key, shape, pieces, -0.22, 0.18)
    return jnp.clip(array, -limit, limit).astype(kind)


def setup_inputs(seed: int = 0, part: int = 0) -> dict:
    seeds = jax.random.split(jax.random.key(seed), 15)
    part_keys = jax.random.split(jax.random.fold_in(seeds[14], part), 15)
    return {
        "latents": noise(part_keys[0], (MICRO, NODES, D), 1.0, 6.0, ((1, 4),)),
        "neighbors": touch_ends(jax.random.randint(part_keys[1], (DEG, NODES), 0, NODE_DEV), jax.random.fold_in(part_keys[1], 1), 0, NODE_DEV - 1).astype(jnp.int32),
        "edge_coef": jnp.clip(jnp.exp(math.log(4.0) - 2.7725887 * jax.random.uniform(part_keys[2], (DEG, NODES), jnp.float32) ** levels(part_keys[2], (DEG, NODES), ((1, 4),), -0.2, 0.2)), 0.25, 4.0),
        "cross_src": touch_ends(jax.random.randint(part_keys[3], (ROUNDS, XDEG, SLOTS), 0, NODE_DEV), jax.random.fold_in(part_keys[3], 1), 0, NODE_DEV - 1).astype(jnp.int32),
        "cross_coef": jnp.clip(jnp.exp(math.log(10.0) - 3.6888795 * jax.random.uniform(part_keys[4], (ROUNDS, XDEG, SLOTS), jnp.float32) ** levels(part_keys[4], (ROUNDS, XDEG, SLOTS), ((2, 4),), -0.2, 0.2)), 0.25, 10.0),
        "recv_node": touch_ends(jax.random.randint(part_keys[5], (ROUNDS, SLOTS), 0, NODE_DEV), jax.random.fold_in(part_keys[5], 1), 0, NODE_DEV - 1).astype(jnp.int32),
        "w_edge": noise(seeds[6], (LAYERS, D, D), D ** -0.5, 0.375, ((0, 2),)),
        "w_node_in": draw_w_node_in(jax.random.fold_in(seeds[14], 71), part),
        "w_node_out": draw_w_node_out(jax.random.fold_in(seeds[14], 71), part),
        "edge_bias": noise(seeds[9], (LAYERS, D), 0.5, 3.0, ((0, 2),)),
        "edge_gain": noise(seeds[10], (LAYERS, D), 1.0, 6.0, ((0, 2),)),
        "node_bias": noise(seeds[11], (LAYERS, D), 0.5, 3.0, ((0, 2), (1, 2))),
        "norm_gain": jnp.clip(1.0 + 0.18 * jax.random.normal(seeds[12], (LAYERS, D), jnp.float32), 0.099609375, 1.8984375).astype(jnp.bfloat16),
        "norm_bias": noise(seeds[13], (LAYERS, D), 0.5, 3.0, ((0, 2),)),
    }


def edge_hidden(table, rows, coefs, gain):
    return jax.nn.relu(table[rows] + coefs[:, None] * gain[None, :])

def apply_layer(latent, layer, w_edge, w_node_in, w_node_out, edge_bias, edge_gain, node_bias, norm_gain, norm_bias, node_rows, edge_coef, cross_rows, cross_coef, dest_rows):
    source = (jnp.dot(latent, w_edge[layer], preferred_element_type=jnp.float32) + edge_bias[layer].astype(jnp.float32)).astype(jnp.bfloat16)
    source = lax.optimization_barrier(source).astype(jnp.float32)
    gain = edge_gain[layer].astype(jnp.float32)
    summed = jnp.zeros(source.shape, jnp.float32)
    for k in range(DEG):
        summed = summed + edge_hidden(source, node_rows[k], edge_coef[k], gain)
    for r in range(ROUNDS):
        partial_sum = jnp.zeros((SLOTS, D), jnp.float32)
        for x in range(XDEG):
            partial_sum = partial_sum + edge_hidden(source, cross_rows[r][x], cross_coef[r, x], gain)
        summed = summed.at[dest_rows[r]].add(partial_sum)
    joined = jnp.concatenate([latent, summed.astype(jnp.bfloat16)], axis=1)
    hidden = jax.nn.relu(jnp.dot(joined, w_node_in[layer], preferred_element_type=jnp.float32) + node_bias[layer].astype(jnp.float32)).astype(jnp.bfloat16)
    half = D // N_CHAN
    mixed = jnp.zeros(source.shape, jnp.float32)
    for g in range(N_CHAN):
        product = jnp.dot(hidden[:, g * half:(g + 1) * half], w_node_out[layer][g * half:(g + 1) * half], preferred_element_type=jnp.float32).astype(jnp.bfloat16)
        mixed = mixed + lax.optimization_barrier(product).astype(jnp.float32)
    mean = lax.optimization_barrier(jnp.mean(mixed, axis=1, keepdims=True))
    centred = mixed - mean
    spread = lax.optimization_barrier(jnp.mean(centred * centred, axis=1, keepdims=True))
    normed = centred * lax.rsqrt(spread + 1e-05) * norm_gain[layer].astype(jnp.float32) + norm_bias[layer].astype(jnp.float32)
    return (latent.astype(jnp.float32) + normed).astype(jnp.bfloat16)

def reference(latents, neighbors, edge_coef, cross_src, cross_coef, recv_node, w_edge, w_node_in, w_node_out, edge_bias, edge_gain, node_bias, norm_gain, norm_bias):
    node_base = (np.arange(NODES) // NODE_DEV * NODE_DEV).astype(np.int32)
    node_rows = neighbors + jnp.asarray(node_base)[None, :]
    slot_part = np.arange(SLOTS) // IFC
    slot_index = np.arange(SLOTS) % IFC
    cross_rows = []
    dest_rows = []
    for r in range(ROUNDS):
        partner = slot_part ^ 1 << r
        columns = jnp.asarray((partner * IFC + slot_index).astype(np.int32))
        dest_rows.append(recv_node[r][columns] + jnp.asarray((partner * NODE_DEV).astype(np.int32)))
        cross_rows.append([cross_src[r, x] + jnp.asarray((slot_part * NODE_DEV).astype(np.int32)) for x in range(XDEG)])
    results = []
    for m in range(MICRO):
        latent = latents[m]
        for layer in range(LAYERS):
            latent = apply_layer(latent, layer, w_edge, w_node_in, w_node_out, edge_bias, edge_gain, node_bias, norm_gain, norm_bias, node_rows, edge_coef, cross_rows, cross_coef, dest_rows)
        results.append(latent)
    return jnp.stack(results, axis=0)
```

```python
import functools

import jax
import jax.numpy as jnp
from jax import lax
from jax.experimental import pallas as pl
from jax.experimental.pallas import tpu as pltpu
from jax.sharding import PartitionSpec as P

F32 = jnp.float32
BF16 = jnp.bfloat16
VMEM = pl.BlockSpec(memory_space=pltpu.VMEM)
SMEM = pl.BlockSpec(memory_space=pltpu.SMEM)
LANES = 128


def dot(a, b):
    return jnp.dot(a, b, preferred_element_type=F32)


def kernel_call(body, outs, operands, flops, smem=1, limit=24):
    return pl.pallas_call(
        body,
        out_shape=outs,
        in_specs=[SMEM] * smem + [VMEM] * (len(operands) - smem),
        out_specs=jax.tree.map(lambda _: VMEM, outs),
        cost_estimate=pl.CostEstimate(flops=flops, bytes_accessed=1 << 16, transcendentals=0),
        compiler_params=pltpu.CompilerParams(vmem_limit_bytes=limit * 1024 * 1024),
    )(*operands)


def shape(dims, dtype):
    return jax.ShapeDtypeStruct(dims, dtype)


def pack_rows(width):
    half = width // 2
    edge, inner, outer, vecs = 0, half, half + width, 2 * half + width
    return edge, inner, outer, vecs, vecs + 16


def pack_kernel(place, w_edge, w_in, w_out, e_bias, e_gain, n_bias, g_norm, b_norm, out):
    layers, width, _ = w_edge.shape
    half = width // 2
    edge, inner, outer, vecs, _ = pack_rows(width)
    mine = pl.multiple_of(place[1] * half, half)
    for j in range(layers):
        out[j, edge : edge + half, :] = w_edge[j, pl.ds(mine, half), :]
        out[j, inner : inner + width, 0:half] = w_in[j, 0:width, :]
        out[j, inner : inner + width, half:width] = w_in[j, width : 2 * width, :]
        out[j, outer : outer + half, :] = w_out[j]
        spot = lax.broadcasted_iota(jnp.int32, (16, width), 0)
        block = jnp.zeros((16, width), F32)
        bias = n_bias[j : j + 1, :].astype(F32)
        rows = [
            e_bias[j : j + 1, :].astype(F32),
            e_gain[j : j + 1, :].astype(F32),
            jnp.concatenate([bias, bias], axis=1),
            g_norm[j : j + 1, :].astype(F32),
            b_norm[j : j + 1, :].astype(F32),
        ]
        for i, row in enumerate(rows):
            block = jnp.where(spot == i, row, block)
        out[j, vecs : vecs + 16, :] = block.astype(BF16)


def columns(rows):
    rows = rows.astype(F32)
    missing = -rows.shape[0] % 8
    if missing:
        rows = jnp.concatenate([rows, jnp.zeros((missing, rows.shape[1]), F32)], axis=0)
    return rows.T


def one_hot_rows(index_columns, coef_columns, count, nodes, hot, spread):
    rows = index_columns.shape[0]
    lane = lax.broadcasted_iota(jnp.int32, (rows, nodes), 1).astype(F32)
    for k in range(count):
        hot[k * rows : (k + 1) * rows, :] = jnp.where(
            index_columns[:, k : k + 1] == lane, 1.0, 0.0
        ).astype(BF16)
        spread[k * rows : (k + 1) * rows, :] = jnp.broadcast_to(
            coef_columns[:, k : k + 1], (rows, LANES)
        )


def cross_prep_kernel(src, coef, recv, hot, spread, scatter):
    rounds, slots = recv.shape
    nodes = hot.shape[1]
    one_hot_rows(columns(src[...]), columns(coef[...]), src.shape[0], nodes, hot, spread)
    row = lax.broadcasted_iota(jnp.int32, (nodes, slots), 0)
    for r in range(rounds):
        scatter[:, r * slots : (r + 1) * slots] = jnp.where(
            recv[r : r + 1, :] == row, 1.0, 0.0
        ).astype(BF16)


def inner_prep_kernel(neighbors, coef, hot, spread):
    one_hot_rows(
        columns(neighbors[...]), columns(coef[...]), neighbors.shape[0], neighbors.shape[1], hot, spread
    )


def wide(spread):
    return jnp.concatenate([spread, spread], axis=1)


def cross_sums(source, gain, hot, spread, outs):
    slots = outs[0].shape[0]
    each = hot.shape[0] // (len(outs) * slots)
    for r, out in enumerate(outs):
        total = None
        for x in range(each):
            rows = pl.ds((r * each + x) * slots, slots)
            hidden = jnp.maximum(dot(hot[rows, :], source) + wide(spread[rows, :]) * gain, 0.0)
            total = hidden if total is None else total + hidden
        out[...] = total.astype(BF16)


def first_sums_kernel(rounds, wave, place, latents, w_edge, e_bias, e_gain, hot, spread, *outs):
    micro = jnp.minimum(wave * 2 + place[1], latents.shape[0] - 1)
    source = (dot(latents[micro], w_edge[0]) + e_bias[0:1, :].astype(F32)).astype(BF16)
    cross_sums(source, e_gain[0:1, :].astype(F32), hot, spread, outs)


def choose(which, refs, j, rows):
    value = refs[0][j, rows, :]
    for r in range(1, len(refs)):
        value = jnp.where(which == r, refs[r][j, rows, :], value)
    return value


def edge_weights(place, which, mine, other, j, width):
    half = width // 2
    edge, _, _, vecs, _ = pack_rows(width)
    a = choose(which, mine, j, slice(edge, edge + half))
    b = choose(which, other, j, slice(edge, edge + half))
    first = place[1] == 0
    weights = jnp.concatenate([jnp.where(first, a, b), jnp.where(first, b, a)], axis=0)
    return weights, choose(which, mine, j, slice(vecs, vecs + 16)).astype(F32)


def inner_kernel(segments, segment, j, first, place, *refs):
    mine, other = refs[:segments], refs[segments : 2 * segments]
    latent, source, hot, spread, sums, before, chosen = refs[2 * segments :]
    nodes, width = sums.shape
    half = width // 2
    _, inner, outer, vecs, _ = pack_rows(width)
    which = lax.rem(place[0] - segment + segments, segments)
    vectors = choose(which, mine, j, slice(vecs, vecs + 16)).astype(F32)
    if first:
        values = latent[place[0]]
        weights, vectors = edge_weights(place, which, mine, other, j, width)
        table = (dot(values, weights) + vectors[0:1, :]).astype(BF16)
    else:
        values = latent[...]
        table = source[...]
    gain = vectors[1:2, :]
    total = None
    for k in range(hot.shape[0] // nodes):
        rows = pl.ds(k * nodes, nodes)
        hidden = jnp.maximum(dot(hot[rows, :], table) + wide(spread[rows, :]) * gain, 0.0)
        total = hidden if total is None else total + hidden
    sums[...] = total
    in_a = choose(which, mine, j, slice(inner, inner + width))
    in_b = choose(which, other, j, slice(inner, inner + width))
    other_vectors = choose(which, other, j, slice(vecs, vecs + 16)).astype(F32)
    bias = jnp.concatenate([vectors[2:3, :half], other_vectors[2:3, :half]], axis=1)
    before[...] = dot(values, jnp.concatenate([in_a[:, :half], in_b[:, :half]], axis=1)) + bias
    chosen[0:width, :] = jnp.concatenate([in_a[:, half:], in_b[:, half:]], axis=1)
    chosen[width : width + half, :] = choose(which, mine, j, slice(outer, outer + half))
    chosen[width + half : 2 * width, :] = choose(which, other, j, slice(outer, outer + half))
    chosen[2 * width : 2 * width + 16, :] = vectors.astype(BF16)


def node_kernel(segments, segment, j, last, many, first, place, *refs):
    arrived, refs = refs[:many], refs[many:]
    latent, sums, before, chosen, scatter = refs[:5]
    nodes, width = sums.shape
    half = width // 2
    rounds = scatter.shape[1] // arrived[0].shape[0]
    per = many // rounds
    blocks = []
    for r in range(rounds):
        block = arrived[r * per][...]
        for i in range(1, per):
            block = block + arrived[r * per + i][...]
        blocks.append(block)
    summed = sums[...] + dot(scatter[...], jnp.concatenate(blocks, axis=0))
    hidden = before[...] + dot(summed.astype(BF16), chosen[0:width, :])
    hidden = jnp.maximum(hidden, 0.0).astype(BF16)
    mixed = dot(hidden[:, :half], chosen[width : width + half, :]).astype(BF16).astype(F32)
    mixed = mixed + dot(hidden[:, half:], chosen[width + half : 2 * width, :]).astype(BF16).astype(F32)
    vectors = chosen[2 * width : 2 * width + 16, :].astype(F32)
    centred = mixed - jnp.mean(mixed, axis=1, keepdims=True)
    spread_of = jnp.mean(centred * centred, axis=1, keepdims=True)
    normed = centred * lax.rsqrt(spread_of + 1e-05) * vectors[3:4, :] + vectors[4:5, :]
    old = latent[place[0]] if first else latent[...]
    fresh = (old.astype(F32) + normed).astype(BF16)
    if last:
        refs[5][0] = fresh
        return
    mine, other = refs[5 : 5 + segments], refs[5 + segments : 5 + 2 * segments]
    hot, spread, result, source = refs[5 + 2 * segments : 9 + 2 * segments]
    outs = refs[9 + 2 * segments :]
    result[...] = fresh
    which = lax.rem(place[0] - segment + segments, segments)
    weights, vectors = edge_weights(place, which, mine, other, j, width)
    table = (dot(fresh, weights) + vectors[0:1, :]).astype(BF16)
    source[...] = table
    cross_sums(table, vectors[1:2, :], hot, spread, outs)


def partner_route(count, r):
    return [(i, i ^ 1 << r) for i in range(count) if i ^ 1 << r < count]


def swap(block):
    return lax.ppermute(block, "chan", [(0, 1), (1, 0)])


def per_device(
    latents,
    neighbors,
    edge_coef,
    cross_src,
    cross_coef,
    recv_node,
    w_edge,
    w_node_in,
    w_node_out,
    edge_bias,
    edge_gain,
    node_bias,
    norm_gain,
    norm_bias,
):
    segments, cores, parts = (lax.axis_size(a) for a in ("segment", "chan", "dom"))
    micro, nodes, width = latents.shape
    held = w_edge.shape[0]
    rounds, slots = recv_node.shape
    degree, edges = neighbors.shape[0], cross_src.shape[0] * cross_src.shape[1]
    assert micro == segments and cores == 2
    place = jnp.stack([lax.axis_index("segment"), lax.axis_index("chan")]).astype(jnp.int32)

    hot_c, spread_c, scatter = kernel_call(
        cross_prep_kernel,
        (shape((edges * slots, nodes), BF16), shape((edges * slots, LANES), F32), shape((nodes, rounds * slots), BF16)),
        (cross_src.reshape(edges, slots), cross_coef.reshape(edges, slots), recv_node),
        1 << 30,
        smem=0,
    )
    packed = kernel_call(
        pack_kernel,
        shape((held, pack_rows(width)[-1], width), BF16),
        (place, w_edge, w_node_in, w_node_out, edge_bias, edge_gain, node_bias, norm_gain, norm_bias),
        1 << 28,
    )

    arrived = [[] for _ in range(rounds)]
    for wave in range(-(-segments // cores)):
        sums = kernel_call(
            functools.partial(first_sums_kernel, rounds, wave),
            [shape((slots, width), BF16)] * rounds,
            (place, latents, w_edge, edge_bias, edge_gain, hot_c, spread_c),
            1 << 29,
        )
        for r in range(rounds):
            route = []
            for here, there in partner_route(parts, r):
                for core in range(cores):
                    goal = wave * cores + core
                    if goal < segments:
                        route.append(
                            (here * segments * cores + core, (there * segments + goal) * cores + core)
                        )
            block = lax.ppermute(sums[r], ("dom", "segment", "chan"), route)
            arrived[r] += [block, swap(block)]

    packs, others = [], []
    for r in range(segments):
        layers = [packed[j : j + 1] for j in range(held)]
        if r:
            route = [(i, (i + r) % segments) for i in range(segments)]
            layers = [lax.ppermute(layer, "segment", route) for layer in layers]
        packs.append(layers)
        others.append([swap(layer) for layer in layers])

    hot, spread = kernel_call(
        inner_prep_kernel,
        (shape((degree * nodes, nodes), BF16), shape((degree * nodes, LANES), F32)),
        (neighbors, edge_coef),
        1 << 31,
        smem=0,
    )

    total = segments * held
    latent, source = latents, None
    for layer in range(total):
        segment, j = divmod(layer, held)
        mine = [packs[r][j] for r in range(segments)]
        other = [others[r][j] for r in range(segments)]
        sums, before, chosen = kernel_call(
            functools.partial(inner_kernel, segments, segment, 0, layer == 0),
            (shape((nodes, width), F32), shape((nodes, width), F32), shape((2 * width + 16, width), BF16)),
            (place, *mine, *other, latent, latent if layer == 0 else source, hot, spread),
            1 << 31,
        )
        blocks = [block for r in range(rounds) for block in arrived[r]]
        last = layer == total - 1
        operands = [place, *blocks, latent, sums, before, chosen, scatter]
        outs = [shape((1, nodes, width), BF16)]
        follow, step = divmod(layer + 1, held)
        if not last:
            operands += [packs[r][step] for r in range(segments)] + [others[r][step] for r in range(segments)]
            operands += [hot_c, spread_c]
            outs = [shape((nodes, width), BF16)] * 2 + [shape((slots, width), BF16)] * rounds
        results = kernel_call(
            functools.partial(node_kernel, segments, follow, 0, last, len(blocks), layer == 0),
            outs,
            operands,
            1 << 30,
        )
        if last:
            return results[0]
        latent, source = results[0], results[1]
        arrived = [
            [lax.ppermute(results[2 + r], "dom", partner_route(parts, r))] for r in range(rounds)
        ]


def solution(mesh):
    return jax.shard_map(
        per_device,
        mesh=mesh,
        in_specs=(
            P(None, ("groups", "dom"), None),
            P(None, ("groups", "dom")),
            P(None, ("groups", "dom")),
            P(None, None, ("groups", "dom")),
            P(None, None, ("groups", "dom")),
            P(None, ("groups", "dom")),
            P("segment", None, None),
            P("segment", None, "chan"),
            P("segment", "chan", None),
            P("segment", None),
            P("segment", None),
            P("segment", "chan"),
            P("segment", None),
            P("segment", None),
        ),
        out_specs=P("segment", ("groups", "dom"), None),
        check_vma=False,
    )
```

```python
import functools

import jax
import jax.numpy as jnp
from jax import lax
from jax.experimental import pallas as pl
from jax.experimental.pallas import tpu as pltpu
from jax.sharding import PartitionSpec as P

F32 = jnp.float32
BF16 = jnp.bfloat16
VMEM = pl.BlockSpec(memory_space=pltpu.VMEM)
SMEM = pl.BlockSpec(memory_space=pltpu.SMEM)
HBM = pl.BlockSpec(memory_space=pltpu.HBM)
LANES = 128


def dot(a, b):
    return jnp.dot(a, b, preferred_element_type=F32)


def kernel_call(body, outs, operands, flops, smem=1, space=VMEM, scratch=(), limit=24):
    return pl.pallas_call(
        body,
        out_shape=outs,
        in_specs=[SMEM] * smem + [space] * (len(operands) - smem),
        out_specs=jax.tree.map(lambda _: VMEM, outs),
        scratch_shapes=scratch,
        cost_estimate=pl.CostEstimate(flops=flops, bytes_accessed=1 << 16, transcendentals=0),
        compiler_params=pltpu.CompilerParams(vmem_limit_bytes=limit * 1024 * 1024),
    )(*operands)


def shape(dims, dtype):
    return jax.ShapeDtypeStruct(dims, dtype)


VECTORS = 16


def start_kernel(
    held,
    waves,
    place,
    latents,
    w_edge,
    w_in,
    w_out,
    e_bias,
    e_gain,
    n_bias,
    g_norm,
    b_norm,
    src,
    coef,
    recv,
    *refs,
):
    edge_whole, edge_pack, *refs = refs
    node_packs, refs = refs[:held], refs[held:]
    latent, early, src_here, coef_here, recv_here, *vectors, sem = refs
    half = w_out.shape[1]
    width = w_out.shape[2]
    mine = pl.multiple_of(place[1] * half, half)
    copies = []

    def fetch(source, target):
        copy = pltpu.make_async_copy(source, target, sem.at[len(copies)])
        copy.start()
        copies.append(copy)

    for ref, here in zip((e_bias, e_gain, n_bias, g_norm, b_norm), vectors):
        fetch(ref, here)
    for j in range(held):
        fetch(w_edge.at[j, pl.ds(mine, half)], edge_pack.at[j, pl.ds(0, half)])
    for j in range(held):
        fetch(w_in.at[j, pl.ds(0, width)], node_packs[j].at[pl.ds(0, width), pl.ds(0, half)])
        fetch(w_in.at[j, pl.ds(width, width)], node_packs[j].at[pl.ds(0, width), pl.ds(half, half)])
        fetch(w_out.at[j], node_packs[j].at[pl.ds(width, half)])
    fetch(src, src_here)
    fetch(coef, coef_here)
    fetch(recv, recv_here)
    for wave in range(waves):
        fetch(latents.at[jnp.minimum(wave * 2 + place[1], latents.shape[0] - 1)], early.at[wave])
    fetch(latents.at[place[0]], latent)
    fetch(w_edge, edge_whole)
    for copy in copies[:5]:
        copy.wait()
    spot = lax.broadcasted_iota(jnp.int32, (VECTORS, width), 0)
    for j in range(held):
        block = jnp.zeros((VECTORS, width), F32)
        for i, here in enumerate(vectors):
            row = here[j : j + 1, :].astype(F32)
            if row.shape[1] == half:
                row = jnp.concatenate([row, row], axis=1)
            block = jnp.where(spot == i, row, block)
        edge_pack[j, half : half + VECTORS, :] = block.astype(BF16)
    for copy in copies[5:]:
        copy.wait()


def columns(rows):
    rows = rows.astype(F32)
    missing = -rows.shape[0] % 8
    if missing:
        rows = jnp.concatenate([rows, jnp.zeros((missing, rows.shape[1]), F32)], axis=0)
    return rows.T


def one_hot_rows(index_columns, coef_columns, count, nodes, hot, spread):
    rows = index_columns.shape[0]
    lane = lax.broadcasted_iota(jnp.int32, (rows, nodes), 1).astype(F32)
    for k in range(count):
        hot[k * rows : (k + 1) * rows, :] = jnp.where(
            index_columns[:, k : k + 1] == lane, 1.0, 0.0
        ).astype(BF16)
        spread[k * rows : (k + 1) * rows, :] = jnp.broadcast_to(
            coef_columns[:, k : k + 1], (rows, LANES)
        )


def first_sums_kernel(rounds, waves, src, coef, recv, early, edge_whole, edge_pack, hot, spread, scatter, *outs):
    slots = recv.shape[1]
    nodes, half = hot.shape[1], edge_pack.shape[1] - VECTORS
    whole = [jnp.concatenate([ref[r] for r in range(rounds)], axis=0) for ref in (src, coef)]
    one_hot_rows(columns(whole[0]), columns(whole[1]), whole[0].shape[0], nodes, hot, spread)
    row = lax.broadcasted_iota(jnp.int32, (nodes, slots), 0)
    for r in range(rounds):
        scatter[:, r * slots : (r + 1) * slots] = jnp.where(recv[r : r + 1, :] == row, 1.0, 0.0).astype(BF16)
    vectors = edge_pack[0, half : half + VECTORS, :].astype(F32)
    for wave in range(waves):
        source = (dot(early[wave], edge_whole[0]) + vectors[0:1, :]).astype(BF16)
        cross_sums(source, vectors[1:2, :], hot, spread, outs[wave * rounds : (wave + 1) * rounds])


def inner_prep_kernel(neighbors, coef, hot, spread, neighbors_here, coef_here, sem):
    copies = [
        pltpu.make_async_copy(neighbors, neighbors_here, sem.at[0]),
        pltpu.make_async_copy(coef, coef_here, sem.at[1]),
    ]
    for copy in copies:
        copy.start()
    for copy in copies:
        copy.wait()
    degree, nodes = neighbors.shape
    one_hot_rows(columns(neighbors_here[...]), columns(coef_here[...]), degree, nodes, hot, spread)


def wide(spread):
    return jnp.concatenate([spread, spread], axis=1)


def cross_sums(source, gain, hot, spread, outs):
    slots = outs[0].shape[0]
    each = hot.shape[0] // (len(outs) * slots)
    for r, out in enumerate(outs):
        total = None
        for x in range(each):
            rows = pl.ds((r * each + x) * slots, slots)
            hidden = jnp.maximum(dot(hot[rows, :], source) + wide(spread[rows, :]) * gain, 0.0)
            total = hidden if total is None else total + hidden
        out[...] = total.astype(BF16)


def choose(which, refs, rows):
    value = refs[0][rows, :]
    for r in range(1, len(refs)):
        value = jnp.where(which == r, refs[r][rows, :], value)
    return value


def edge_weights(place, which, j, edge_whole, mine, other):
    half = mine[0].shape[1] - VECTORS
    first = place[1] == 0
    weights = edge_whole[j]
    vectors = mine[0][j, half : half + VECTORS, :]
    for r in range(1, len(mine)):
        a, b = mine[r][j, 0:half, :], other[r - 1][j, 0:half, :]
        halves = jnp.concatenate([jnp.where(first, a, b), jnp.where(first, b, a)], axis=0)
        weights = jnp.where(which == r, halves, weights)
        vectors = jnp.where(which == r, mine[r][j, half : half + VECTORS, :], vectors)
    return weights, vectors.astype(F32)


def place_of(segment, segments, place):
    return lax.rem(place[0] - segment + segments, segments)


def inner_kernel(segments, segment, j, first, place, edge_whole, *refs):
    mine, other = refs[:segments], refs[segments : 2 * segments - 1]
    table, hot, spread, sums = refs[2 * segments - 1 :]
    nodes = sums.shape[0]
    which = place_of(segment, segments, place)
    weights, vectors = edge_weights(place, which, j, edge_whole, mine, other)
    values = table[...]
    if first:
        values = (dot(values, weights) + vectors[0:1, :]).astype(BF16)
    gain = vectors[1:2, :]
    total = None
    for k in range(hot.shape[0] // nodes):
        rows = pl.ds(k * nodes, nodes)
        hidden = jnp.maximum(dot(hot[rows, :], values) + wide(spread[rows, :]) * gain, 0.0)
        total = hidden if total is None else total + hidden
    sums[...] = total


def weights_kernel(segments, segment, j, place, *refs):
    mine, other = refs[:segments], refs[segments : 2 * segments]
    vec_mine, vec_other = refs[2 * segments : 3 * segments], refs[3 * segments : 4 * segments]
    latent, before, chosen = refs[4 * segments :]
    width = before.shape[1]
    half = width // 2
    which = place_of(segment, segments, place)
    in_a, in_b = (choose(which, refs, slice(0, width)) for refs in (mine, other))
    vectors, other_vectors = (
        choose(which, [ref.at[j] for ref in refs], slice(half, half + VECTORS)).astype(F32)
        for refs in (vec_mine, vec_other)
    )
    bias = jnp.concatenate([vectors[2:3, :half], other_vectors[2:3, :half]], axis=1)
    joined = jnp.concatenate([in_a[:, :half], in_b[:, :half]], axis=1)
    before[...] = dot(latent[...], joined) + bias
    chosen[0:width, :] = jnp.concatenate([in_a[:, half:], in_b[:, half:]], axis=1)
    chosen[width : width + half, :] = choose(which, mine, slice(width, width + half))
    chosen[width + half : 2 * width, :] = choose(which, other, slice(width, width + half))
    chosen[2 * width : 2 * width + VECTORS, :] = vectors.astype(BF16)


def node_kernel(segments, segment, j, last, many, place, *refs):
    arrived, refs = refs[:many], refs[many:]
    latent, sums, before, chosen, scatter = refs[:5]
    nodes, width = sums.shape
    half = width // 2
    rounds = scatter.shape[1] // arrived[0].shape[0]
    per = many // rounds
    blocks = []
    for r in range(rounds):
        block = arrived[r * per][...]
        for i in range(1, per):
            block = block + arrived[r * per + i][...]
        blocks.append(block)
    summed = sums[...] + dot(scatter[...], jnp.concatenate(blocks, axis=0))
    hidden = before[...] + dot(summed.astype(BF16), chosen[0:width, :])
    hidden = jnp.maximum(hidden, 0.0).astype(BF16)
    mixed = dot(hidden[:, :half], chosen[width : width + half, :]).astype(BF16).astype(F32)
    mixed = mixed + dot(hidden[:, half:], chosen[width + half : 2 * width, :]).astype(BF16).astype(F32)
    vectors = chosen[2 * width : 2 * width + VECTORS, :].astype(F32)
    centred = mixed - jnp.mean(mixed, axis=1, keepdims=True)
    spread_of = jnp.mean(centred * centred, axis=1, keepdims=True)
    normed = centred * lax.rsqrt(spread_of + 1e-05) * vectors[3:4, :] + vectors[4:5, :]
    fresh = (latent[...].astype(F32) + normed).astype(BF16)
    if last:
        refs[5][0] = fresh
        return
    edge_whole, *refs = refs[5:]
    mine, other, refs = refs[:segments], refs[segments : 2 * segments - 1], refs[2 * segments - 1 :]
    hot, spread, result, source = refs[:4]
    result[...] = fresh
    which = place_of(segment, segments, place)
    weights, vectors = edge_weights(place, which, j, edge_whole, mine, other)
    table = (dot(fresh, weights) + vectors[0:1, :]).astype(BF16)
    source[...] = table
    cross_sums(table, vectors[1:2, :], hot, spread, refs[4:])


def partner_route(count, r):
    return [(i, i ^ 1 << r) for i in range(count) if i ^ 1 << r < count]


def swap(block):
    return lax.ppermute(block, "chan", [(0, 1), (1, 0)])


def per_device(
    latents,
    neighbors,
    edge_coef,
    cross_src,
    cross_coef,
    recv_node,
    w_edge,
    w_node_in,
    w_node_out,
    edge_bias,
    edge_gain,
    node_bias,
    norm_gain,
    norm_bias,
):
    segments, cores, parts = (lax.axis_size(a) for a in ("segment", "chan", "dom"))
    micro, nodes, width = latents.shape
    held = w_edge.shape[0]
    rounds, slots = recv_node.shape
    degree, edges = neighbors.shape[0], cross_src.shape[0] * cross_src.shape[1]
    assert micro == segments and cores == 2
    place = jnp.stack([lax.axis_index("segment"), lax.axis_index("chan")]).astype(jnp.int32)

    waves = -(-segments // cores)
    half = width // 2
    vectors = (edge_bias, edge_gain, node_bias, norm_gain, norm_bias)
    graph = (cross_src, cross_coef, recv_node)
    outs = [shape((held, width, width), BF16), shape((held, half + VECTORS, width), BF16)]
    outs += [shape((width + half, width), BF16)] * held
    outs += [shape((nodes, width), BF16), shape((waves, nodes, width), BF16)]
    outs += [shape(ref.shape, ref.dtype) for ref in graph]
    edge_whole, edge_pack, *rest = kernel_call(
        functools.partial(start_kernel, held, waves),
        outs,
        (place, *map(lambda v: pltpu.with_memory_space_constraint(v, pltpu.HBM), (latents, w_edge, w_node_in, w_node_out, *vectors, *graph))),
        1 << 28,
        space=HBM,
        scratch=[pltpu.VMEM(ref.shape, ref.dtype) for ref in vectors]
        + [pltpu.SemaphoreType.DMA((5 + 4 * held + 3 + waves + 2,))],
    )
    node_packs, (latent, early, *graph) = rest[:held], rest[held:]

    hot_c, spread_c, scatter, *sums = kernel_call(
        functools.partial(first_sums_kernel, rounds, waves),
        [shape((edges * slots, nodes), BF16), shape((edges * slots, LANES), F32), shape((nodes, rounds * slots), BF16)]
        + [shape((slots, width), BF16)] * (waves * rounds),
        (*graph, early, edge_whole, edge_pack),
        1 << 29,
        smem=0,
    )
    arrived = [[] for _ in range(rounds)]
    for wave in range(waves):
        for r in range(rounds):
            route = []
            for here, there in partner_route(parts, r):
                for core in range(cores):
                    goal = wave * cores + core
                    if goal < segments:
                        route.append(
                            (here * segments * cores + core, (there * segments + goal) * cores + core)
                        )
            block = lax.ppermute(sums[wave * rounds + r], ("dom", "segment", "chan"), route)
            arrived[r] += [block, swap(block)]

    edges_mine, nodes_mine = [edge_pack], [node_packs]
    for r in range(1, segments):
        route = [(i, (i + r) % segments) for i in range(segments)]
        edges_mine.append(lax.ppermute(edge_pack, "segment", route))
        nodes_mine.append([lax.ppermute(pack, "segment", route) for pack in node_packs])
    edges_other = [swap(pack) for pack in edges_mine]
    nodes_other = [[swap(pack) for pack in packs] for packs in nodes_mine]

    hot, spread = kernel_call(
        inner_prep_kernel,
        (shape((degree * nodes, nodes), BF16), shape((degree * nodes, LANES), F32)),
        tuple(pltpu.with_memory_space_constraint(v, pltpu.HBM) for v in (neighbors, edge_coef)),
        1 << 31,
        smem=0,
        space=HBM,
        scratch=[
            pltpu.VMEM(neighbors.shape, neighbors.dtype),
            pltpu.VMEM(edge_coef.shape, edge_coef.dtype),
            pltpu.SemaphoreType.DMA((2,)),
        ],
    )

    total = segments * held
    source = latent
    for layer in range(total):
        segment, j = divmod(layer, held)
        edge_operands = (edge_whole, *edges_mine, *edges_other[1:])
        sums = kernel_call(
            functools.partial(inner_kernel, segments, segment, j, layer == 0),
            shape((nodes, width), F32),
            (place, *edge_operands, source, hot, spread),
            1 << 31,
        )
        before, chosen = kernel_call(
            functools.partial(weights_kernel, segments, segment, j),
            (shape((nodes, width), F32), shape((2 * width + VECTORS, width), BF16)),
            (
                place,
                *[packs[j] for packs in nodes_mine],
                *[packs[j] for packs in nodes_other],
                *edges_mine,
                *edges_other,
                latent,
            ),
            1 << 28,
        )
        blocks = [block for r in range(rounds) for block in arrived[r]]
        last = layer == total - 1
        operands = [place, *blocks, latent, sums, before, chosen, scatter]
        outs = [shape((1, nodes, width), BF16)]
        follow, step = divmod(layer + 1, held)
        if not last:
            operands += [*edge_operands, hot_c, spread_c]
            outs = [shape((nodes, width), BF16)] * 2 + [shape((slots, width), BF16)] * rounds
        results = kernel_call(
            functools.partial(node_kernel, segments, follow, step, last, len(blocks)),
            outs,
            operands,
            1 << 30,
        )
        if last:
            return results[0]
        latent, source, *blocks = results
        arrived = [[lax.ppermute(blocks[r], "dom", partner_route(parts, r))] for r in range(rounds)]


def solution(mesh):
    return jax.shard_map(
        per_device,
        mesh=mesh,
        in_specs=(
            P(None, ("groups", "dom"), None),
            P(None, ("groups", "dom")),
            P(None, ("groups", "dom")),
            P(None, None, ("groups", "dom")),
            P(None, None, ("groups", "dom")),
            P(None, ("groups", "dom")),
            P("segment", None, None),
            P("segment", None, "chan"),
            P("segment", "chan", None),
            P("segment", None),
            P("segment", None),
            P("segment", "chan"),
            P("segment", None),
            P("segment", None),
        ),
        out_specs=P("segment", ("groups", "dom"), None),
        check_vma=False,
    )
```

```python
import functools

import jax
import jax.numpy as jnp
from jax import lax
from jax.experimental import pallas as pl
from jax.experimental.pallas import tpu as pltpu
from jax.sharding import PartitionSpec as P

F32 = jnp.float32
BF16 = jnp.bfloat16
VMEM = pl.BlockSpec(memory_space=pltpu.VMEM)
SMEM = pl.BlockSpec(memory_space=pltpu.SMEM)
HBM = pl.BlockSpec(memory_space=pltpu.HBM)
ANY = pl.BlockSpec(memory_space=pl.ANY)
LANES = 128


def dot(a, b):
    return jnp.dot(a, b, preferred_element_type=F32)


def kernel_call(body, outs, operands, flops, smem=1, scratch=(), after=0):
    plain = len(operands) - smem - after
    return pl.pallas_call(
        body,
        out_shape=outs,
        in_specs=[SMEM] * smem + [HBM if scratch else VMEM] * plain + [ANY] * after,
        out_specs=jax.tree.map(lambda _: VMEM, outs),
        scratch_shapes=scratch,
        cost_estimate=pl.CostEstimate(flops=flops, bytes_accessed=1 << 16, transcendentals=0),
        compiler_params=pltpu.CompilerParams(vmem_limit_bytes=24 * 1024 * 1024),
    )(*operands)


def shape(dims, dtype):
    return jax.ShapeDtypeStruct(dims, dtype)


VECTORS = 16


def fetch_all(pairs, sem):
    copies = [pltpu.make_async_copy(a, b, sem.at[i]) for i, (a, b) in enumerate(pairs)]
    for copy in copies:
        copy.start()
    return copies


def vector_rows(rows, width):
    spot = lax.broadcasted_iota(jnp.int32, (VECTORS, width), 0)
    block = jnp.zeros((VECTORS, width), F32)
    for i, row in enumerate(rows):
        row = row.astype(F32)
        if row.shape[1] < width:
            row = jnp.concatenate([row] * (width // row.shape[1]), axis=1)
        block = jnp.where(spot == i, row, block)
    return block.astype(BF16)


def edge_rows(width, j):
    half = width // 2
    start = j * (half + VECTORS)
    return slice(start, start + half), slice(start + half, start + half + VECTORS)


def node_rows(width, held, j):
    half = width // 2
    start = 0 if j else edge_rows(width, held)[0].start
    return slice(start, start + width), slice(start + width, start + width + half)


def pack_kernel(place, w_edge, w_in, w_out, e_bias, e_gain, g_norm, b_norm, n_bias, *refs):
    held, half, width = w_out.shape
    packs, vectors, sem = refs[:held], refs[held:-1], refs[-1]
    mine = pl.multiple_of(place[1] * half, half)
    pairs = list(zip((e_bias, e_gain, g_norm, b_norm, n_bias), vectors))
    for j in range(held):
        inner, outer = node_rows(width, held, j)
        pairs += [
            (w_edge.at[j, pl.ds(mine, half)], packs[0].at[edge_rows(width, j)[0]]),
            (w_in.at[j, pl.ds(0, width)], packs[j].at[inner, pl.ds(0, half)]),
            (w_in.at[j, pl.ds(width, width)], packs[j].at[inner, pl.ds(half, half)]),
            (w_out.at[j], packs[j].at[outer]),
        ]
    copies = fetch_all(pairs, sem)
    for copy in copies[:5]:
        copy.wait()
    for j in range(held):
        packs[0][edge_rows(width, j)[1], :] = vector_rows([ref[j : j + 1, :] for ref in vectors], width)
    for copy in copies[5:]:
        copy.wait()


def columns(rows):
    rows = rows.astype(F32)
    missing = -rows.shape[0] % 8
    if missing:
        rows = jnp.concatenate([rows, jnp.zeros((missing, rows.shape[1]), F32)], axis=0)
    return rows.T


def one_hot_rows(index_columns, coef_columns, count, nodes, hot, spread):
    rows = index_columns.shape[0]
    lane = lax.broadcasted_iota(jnp.int32, (rows, nodes), 1).astype(F32)
    for k in range(count):
        hot[k * rows : (k + 1) * rows, :] = jnp.where(
            index_columns[:, k : k + 1] == lane, 1.0, 0.0
        ).astype(BF16)
        spread[k * rows : (k + 1) * rows, :] = jnp.broadcast_to(
            coef_columns[:, k : k + 1], (rows, LANES)
        )


def pieces(values):
    high = values.astype(BF16)
    rest = values - high.astype(F32)
    middle = rest.astype(BF16)
    return high, middle, (rest - middle.astype(F32)).astype(BF16)


def cross_prep_kernel(place, latents, src, coef, recv, _, latent, hot, spread, scatter, *refs):
    rounds, slots = recv.shape
    raw, here, sem = refs[0], refs[1:4], refs[4]
    copies = fetch_all([*zip((src, coef, recv), here), (latents.at[place[0]], latent)], sem)
    for copy in copies[:3]:
        copy.wait()
    nodes, width = latent.shape
    whole = [jnp.concatenate([ref[r] for r in range(rounds)], axis=0) for ref in here[:2]]
    one_hot_rows(columns(whole[0]), columns(whole[1]), whole[0].shape[0], nodes, hot, spread)
    row = lax.broadcasted_iota(jnp.int32, (nodes, slots), 0)
    for r in range(rounds):
        scatter[:, r * slots : (r + 1) * slots] = jnp.where(
            here[2][r : r + 1, :] == row, 1.0, 0.0
        ).astype(BF16)
    copies[3].wait()
    each = src.shape[1] * slots
    mine = pl.multiple_of(place[1] * each, each)
    raw[0:each, :] = dot(hot[pl.ds(mine, each), :], latent[...]).astype(BF16)
    coefs = here[1][place[1]]
    rows = [piece[x : x + 1, :] for x in range(src.shape[1]) for piece in pieces(coefs)]
    raw[each : each + VECTORS, :] = vector_rows(rows, width)


def inner_prep_kernel(neighbors, coef, _, hot, spread, neighbors_here, coef_here, sem):
    for copy in fetch_all([(neighbors, neighbors_here), (coef, coef_here)], sem):
        copy.wait()
    degree, nodes = neighbors.shape
    one_hot_rows(columns(neighbors_here[...]), columns(coef_here[...]), degree, nodes, hot, spread)


def wide(spread):
    return jnp.concatenate([spread, spread], axis=1)


def cross_sums(source, gain, hot, spread, outs):
    slots = outs[0].shape[0]
    each = hot.shape[0] // (len(outs) * slots)
    for r, out in enumerate(outs):
        total = None
        for x in range(each):
            rows = pl.ds((r * each + x) * slots, slots)
            hidden = jnp.maximum(dot(hot[rows, :], source) + wide(spread[rows, :]) * gain, 0.0)
            total = hidden if total is None else total + hidden
        out[...] = total.astype(BF16)


def choose(which, refs, rows):
    value = refs[0][rows, :]
    for r in range(1, len(refs)):
        value = jnp.where(which == r, refs[r][rows, :], value)
    return value


def place_of(segment, segments, place):
    return lax.rem(place[0] - segment + segments, segments)


def edge_weights(place, which, j, mine, other, width):
    edge, under = edge_rows(width, j)
    a, b = (choose(which, refs, edge) for refs in (mine, other))
    first = place[1] == 0
    weights = jnp.concatenate([jnp.where(first, a, b), jnp.where(first, b, a)], axis=0)
    return weights, choose(which, mine, under).astype(F32)


def send_side(place, which, j, mine, other, latent, hot, spread, source, outs):
    weights, vectors = edge_weights(place, which, j, mine, other, latent.shape[1])
    table = (dot(latent, weights) + vectors[0:1, :]).astype(BF16)
    source[...] = table
    cross_sums(table, vectors[1:2, :], hot, spread, outs)


def partner_sums_kernel(segments, place, *refs):
    mine, other = refs[:segments], refs[segments : 2 * segments]
    raw, outs = refs[2 * segments : 2 * segments + 2], refs[2 * segments + 2 :]
    slots, width = outs[0].shape
    each = (raw[0].shape[0] - VECTORS) // slots
    weights, vectors = edge_weights(place, place_of(0, segments, place), 0, mine, other, width)
    for r, out in enumerate(outs):
        block = jnp.where(place[1] == r, raw[0][...], raw[1][...])
        table = (dot(block[0 : each * slots, :], weights) + vectors[0:1, :]).astype(BF16).astype(F32)
        rows = block[each * slots :, 0:slots].astype(F32)
        coefs = [sum(rows[i : i + 1] for i in range(3 * x + 1, 3 * x + 3)) + rows[3 * x : 3 * x + 1] for x in range(each)]
        coefs = columns(jnp.concatenate(coefs, axis=0))
        total = None
        for x in range(each):
            hidden = table[x * slots : (x + 1) * slots] + coefs[:, x : x + 1] * vectors[1:2, :]
            hidden = jnp.maximum(hidden, 0.0)
            total = hidden if total is None else total + hidden
        out[...] = total.astype(BF16)


def inner_kernel(segments, segment, j, first, place, *refs):
    mine, other = refs[:segments], refs[segments : 2 * segments]
    source, hot, spread, sums = refs[2 * segments :]
    nodes, width = sums.shape
    which = place_of(segment, segments, place)
    table = source[...]
    if first:
        weights, vectors = edge_weights(place, which, j, mine, other, width)
        table = (dot(table, weights) + vectors[0:1, :]).astype(BF16)
    gain = choose(which, mine, edge_rows(width, j)[1]).astype(F32)[1:2, :]
    total = None
    for k in range(hot.shape[0] // nodes):
        rows = pl.ds(k * nodes, nodes)
        hidden = jnp.maximum(dot(hot[rows, :], table) + wide(spread[rows, :]) * gain, 0.0)
        total = hidden if total is None else total + hidden
    sums[...] = total


def weights_kernel(segments, held, segment, j, place, *refs):
    mine, other, vec_mine, vec_other = (refs[i * segments : (i + 1) * segments] for i in range(4))
    latent, before, chosen = refs[4 * segments :]
    width = before.shape[1]
    half = width // 2
    inner, outer = node_rows(width, held, j)
    which = place_of(segment, segments, place)
    in_a, in_b = (choose(which, refs, inner) for refs in (mine, other))
    vec_a, vec_b = (choose(which, refs, edge_rows(width, j)[1]) for refs in (vec_mine, vec_other))
    joined = jnp.concatenate([in_a[:, :half], in_b[:, :half]], axis=1)
    bias = jnp.concatenate([vec_a[:, :half], vec_b[:, :half]], axis=1).astype(F32)[4:5, :]
    before[...] = dot(latent[...], joined) + bias
    chosen[0:width, :] = jnp.concatenate([in_a[:, half:], in_b[:, half:]], axis=1)
    chosen[width : width + half, :] = choose(which, mine, outer)
    chosen[width + half : 2 * width, :] = choose(which, other, outer)
    chosen[2 * width : 2 * width + VECTORS, :] = vec_a


def node_kernel(segments, segment, j, last, rounds, place, *refs):
    arrived, refs = refs[:rounds], refs[rounds:]
    latent, sums, before, chosen, scatter = refs[:5]
    width = sums.shape[1]
    half = width // 2
    summed = sums[...] + dot(scatter[...], jnp.concatenate([block[...] for block in arrived[::-1]], axis=0))
    hidden = before[...] + dot(summed.astype(BF16), chosen[0:width, :])
    hidden = jnp.maximum(hidden, 0.0).astype(BF16)
    mixed = dot(hidden[:, :half], chosen[width : width + half, :]).astype(BF16).astype(F32)
    mixed = mixed + dot(hidden[:, half:], chosen[width + half : 2 * width, :]).astype(BF16).astype(F32)
    vectors = chosen[2 * width : 2 * width + VECTORS, :].astype(F32)
    centred = mixed - jnp.mean(mixed, axis=1, keepdims=True)
    spread_of = jnp.mean(centred * centred, axis=1, keepdims=True)
    normed = centred * lax.rsqrt(spread_of + 1e-05) * vectors[2:3, :] + vectors[3:4, :]
    fresh = (latent[...].astype(F32) + normed).astype(BF16)
    if last:
        refs[5][0] = fresh
        return
    mine, other = refs[5 : 5 + segments], refs[5 + segments : 5 + 2 * segments]
    hot, spread, result, source, *outs = refs[5 + 2 * segments :]
    result[...] = fresh
    which = place_of(segment, segments, place)
    send_side(place, which, j, mine, other, fresh, hot, spread, source, outs)


def partner_route(count, r):
    return [(i, i ^ 1 << r) for i in range(count) if i ^ 1 << r < count]


def per_device(
    latents,
    neighbors,
    edge_coef,
    cross_src,
    cross_coef,
    recv_node,
    w_edge,
    w_node_in,
    w_node_out,
    edge_bias,
    edge_gain,
    node_bias,
    norm_gain,
    norm_bias,
):
    segments, cores, parts = (lax.axis_size(a) for a in ("segment", "chan", "dom"))
    micro, nodes, width = latents.shape
    held = w_edge.shape[0]
    rounds, slots = recv_node.shape
    degree, edges = neighbors.shape[0], cross_src.shape[0] * cross_src.shape[1]
    half = width // 2
    assert micro == segments and cores == rounds == 2
    place = jnp.stack([lax.axis_index("segment"), lax.axis_index("chan")]).astype(jnp.int32)

    def in_hbm(*arrays):
        return [pltpu.with_memory_space_constraint(array, pltpu.HBM) for array in arrays]

    def buffers(*arrays):
        return [pltpu.VMEM(array.shape, array.dtype) for array in arrays]

    def swap(block):
        return lax.ppermute(block, "chan", [(0, 1), (1, 0)])

    def exchange(blocks):
        return [lax.ppermute(block, "dom", partner_route(parts, r)) for r, block in enumerate(blocks)]

    def once(arrays, made):
        return lax.optimization_barrier((arrays, made))[0]

    vectors = (edge_bias, edge_gain, norm_gain, norm_bias, node_bias)
    packs = kernel_call(
        pack_kernel,
        [shape((node_rows(width, held, j)[1].stop, width), BF16) for j in range(held)],
        [place, *in_hbm(w_edge, w_node_in, w_node_out, *vectors)],
        1 << 10,
        scratch=[*buffers(*vectors), pltpu.SemaphoreType.DMA((5 + 4 * held,))],
    )
    graph = (cross_src, cross_coef, recv_node)
    latent, hot_c, spread_c, scatter, raw = kernel_call(
        cross_prep_kernel,
        [
            shape((nodes, width), BF16),
            shape((edges * slots, nodes), BF16),
            shape((edges * slots, LANES), F32),
            shape((nodes, rounds * slots), BF16),
            shape((edges // rounds * slots + VECTORS, width), BF16),
        ],
        [place, *in_hbm(latents, *graph), packs[0]],
        1 << 10,
        after=1,
        scratch=[*buffers(*graph), pltpu.SemaphoreType.DMA((4,))],
    )
    route = []
    for core in range(cores):
        route += [(a * cores + core, b * cores + core) for a, b in partner_route(parts, core)]
    raw = lax.ppermute(raw, ("dom", "chan"), route)
    hot, spread = kernel_call(
        inner_prep_kernel,
        [shape((degree * nodes, nodes), BF16), shape((degree * nodes, LANES), F32)],
        [*in_hbm(neighbors, edge_coef), scatter],
        1 << 30,
        smem=0,
        after=1,
        scratch=[*buffers(neighbors, edge_coef), pltpu.SemaphoreType.DMA((2,))],
    )
    routes = [[(i, (i + r) % segments) for i in range(segments)] for r in range(1, segments)]
    mine_of, other_of = [], []
    for j in range(held):
        ready = once(packs[j], scatter if j else latents)
        mine_of.append([packs[j], *[lax.ppermute(ready, "segment", route) for route in routes]])

    total = segments * held
    sends = [shape((nodes, width), BF16)] + [shape((slots, width), BF16)] * rounds
    def swaps(j, made):
        return [swap(once(packs[j], scatter)), *map(swap, once(mine_of[j][1:], made))]

    source = latent
    for layer in range(total):
        segment, j = divmod(layer, held)
        if layer == 0:
            other_of.append(swaps(0, (raw, hot)))
        weights = [*mine_of[0], *other_of[0]]
        sums = kernel_call(
            functools.partial(inner_kernel, segments, segment, j, layer == 0),
            shape((nodes, width), F32),
            [place, *weights, source, hot, spread],
            1 << 31,
        )
        before, chosen = kernel_call(
            functools.partial(weights_kernel, segments, held, segment, j),
            [shape((nodes, width), F32), shape((2 * width + VECTORS, width), BF16)],
            [place, *mine_of[j], *other_of[j], *weights, latent],
            1 << 28,
        )
        if layer == 0:
            arrived = kernel_call(
                functools.partial(partner_sums_kernel, segments),
                sends[1:],
                [place, *weights, raw, swap(raw)],
                1 << 28,
            )
        else:
            arrived = exchange(blocks)
        operands = [place, *arrived[::-1], latent, sums, before, chosen, scatter]
        last = layer == total - 1
        follow, step = divmod(layer + 1, held)
        if last:
            outs = [shape((1, nodes, width), BF16)]
        else:
            operands += [*weights, hot_c, spread_c]
            outs = [shape((nodes, width), BF16), *sends]
        latent, *rest = kernel_call(
            functools.partial(node_kernel, segments, follow, step, last, rounds), outs, operands, 1 << 30
        )
        if not last:
            source, *blocks = rest
        if layer + 1 < held:
            other_of.append(swaps(layer + 1, source))
    return latent


def solution(mesh):
    return jax.shard_map(
        per_device,
        mesh=mesh,
        in_specs=(
            P(None, ("groups", "dom"), None),
            P(None, ("groups", "dom")),
            P(None, ("groups", "dom")),
            P(None, None, ("groups", "dom")),
            P(None, None, ("groups", "dom")),
            P(None, ("groups", "dom")),
            P("segment", None, None),
            P("segment", None, "chan"),
            P("segment", "chan", None),
            P("segment", None),
            P("segment", None),
            P("segment", "chan"),
            P("segment", None),
            P("segment", None),
        ),
        out_specs=P("segment", ("groups", "dom"), None),
        check_vma=False,
    )
```

```python
import functools

import jax
import jax.numpy as jnp
from jax import lax
from jax.experimental import pallas as pl
from jax.experimental.pallas import tpu as pltpu
from jax.sharding import PartitionSpec as P

F32 = jnp.float32
BF16 = jnp.bfloat16
VMEM = pl.BlockSpec(memory_space=pltpu.VMEM)
HBM = pl.BlockSpec(memory_space=pltpu.HBM)
ANY = pl.BlockSpec(memory_space=pl.ANY)
LANES = 128


def dot(a, b):
    return jnp.dot(a, b, preferred_element_type=F32)


def kernel_call(body, outs, operands, flops, scratch=(), after=0):
    plain = len(operands) - after
    return pl.pallas_call(
        body,
        out_shape=outs,
        in_specs=[HBM if scratch else VMEM] * plain + [ANY] * after,
        out_specs=jax.tree.map(lambda _: VMEM, outs),
        scratch_shapes=scratch,
        cost_estimate=pl.CostEstimate(flops=flops, bytes_accessed=1 << 16, transcendentals=0),
        compiler_params=pltpu.CompilerParams(vmem_limit_bytes=24 * 1024 * 1024),
    )(*operands)


def shape(dims, dtype):
    return jax.ShapeDtypeStruct(dims, dtype)


VECTORS = 16


def fetch_all(pairs, sem):
    copies = [pltpu.make_async_copy(a, b, sem.at[i]) for i, (a, b) in enumerate(pairs)]
    for copy in copies:
        copy.start()
    return copies


def vector_rows(rows, width):
    spot = lax.broadcasted_iota(jnp.int32, (VECTORS, width), 0)
    block = jnp.zeros((VECTORS, width), F32)
    for i, row in enumerate(rows):
        row = row.astype(F32)
        if row.shape[1] < width:
            row = jnp.concatenate([row] * (width // row.shape[1]), axis=1)
        block = jnp.where(spot == i, row, block)
    return block.astype(BF16)


def edge_rows(width, j):
    half = width // 2
    start = j * (half + VECTORS)
    return slice(start, start + half), slice(start + half, start + half + VECTORS)


def node_rows(width, held, j):
    half = width // 2
    start = 0 if j else edge_rows(width, held)[0].start
    return slice(start, start + width), slice(start + width, start + width + half)


def pack_kernel(w_edge, w_in, w_out, e_bias, e_gain, g_norm, b_norm, n_bias, *refs):
    held, half, width = w_out.shape
    packs, vectors, sem = refs[:held], refs[held:-1], refs[-1]
    mine = pl.multiple_of(lax.axis_index("chan") * half, half)
    pairs = list(zip((e_bias, e_gain, g_norm, b_norm, n_bias), vectors))
    for j in range(held):
        inner, outer = node_rows(width, held, j)
        pairs += [
            (w_edge.at[j, pl.ds(mine, half)], packs[0].at[edge_rows(width, j)[0]]),
            (w_in.at[j, pl.ds(0, width)], packs[j].at[inner, pl.ds(0, half)]),
            (w_in.at[j, pl.ds(width, width)], packs[j].at[inner, pl.ds(half, half)]),
            (w_out.at[j], packs[j].at[outer]),
        ]
    copies = fetch_all(pairs, sem)
    for copy in copies[:5]:
        copy.wait()
    for j in range(held):
        packs[0][edge_rows(width, j)[1], :] = vector_rows([ref[j : j + 1, :] for ref in vectors], width)
    for copy in copies[5:]:
        copy.wait()


def columns(rows):
    rows = rows.astype(F32)
    missing = -rows.shape[0] % 8
    if missing:
        rows = jnp.concatenate([rows, jnp.zeros((missing, rows.shape[1]), F32)], axis=0)
    return rows.T


def one_hot_rows(index_columns, coef_columns, count, nodes, hot, spread):
    rows = index_columns.shape[0]
    lane = lax.broadcasted_iota(jnp.int32, (rows, nodes), 1).astype(F32)
    for k in range(count):
        hot[k * rows : (k + 1) * rows, :] = jnp.where(
            index_columns[:, k : k + 1] == lane, 1.0, 0.0
        ).astype(BF16)
        spread[k * rows : (k + 1) * rows, :] = jnp.broadcast_to(
            coef_columns[:, k : k + 1], (rows, LANES)
        )


def pieces(values):
    high = values.astype(BF16)
    rest = values - high.astype(F32)
    middle = rest.astype(BF16)
    return high, middle, (rest - middle.astype(F32)).astype(BF16)


def cross_prep_kernel(latents, src, coef, recv, _, latent, hot, spread, scatter, *refs):
    rounds, slots = recv.shape
    raw, here, sem = refs[0], refs[1:4], refs[4]
    copies = fetch_all([*zip((src, coef, recv), here), (latents.at[lax.axis_index("segment")], latent)], sem)
    for copy in copies[:3]:
        copy.wait()
    nodes, width = latent.shape
    whole = [jnp.concatenate([ref[r] for r in range(rounds)], axis=0) for ref in here[:2]]
    one_hot_rows(columns(whole[0]), columns(whole[1]), whole[0].shape[0], nodes, hot, spread)
    row = lax.broadcasted_iota(jnp.int32, (nodes, slots), 0)
    for r in range(rounds):
        scatter[:, r * slots : (r + 1) * slots] = jnp.where(
            here[2][r : r + 1, :] == row, 1.0, 0.0
        ).astype(BF16)
    copies[3].wait()
    each = src.shape[1] * slots
    mine = pl.multiple_of(lax.axis_index("chan") * each, each)
    raw[0:each, :] = dot(hot[pl.ds(mine, each), :], latent[...]).astype(BF16)
    coefs = here[1][lax.axis_index("chan")]
    rows = [piece[x : x + 1, :] for x in range(src.shape[1]) for piece in pieces(coefs)]
    raw[each : each + VECTORS, :] = vector_rows(rows, width)


def inner_prep_kernel(neighbors, coef, _, hot, spread, neighbors_here, coef_here, sem):
    for copy in fetch_all([(neighbors, neighbors_here), (coef, coef_here)], sem):
        copy.wait()
    degree, nodes = neighbors.shape
    one_hot_rows(columns(neighbors_here[...]), columns(coef_here[...]), degree, nodes, hot, spread)


def wide(spread):
    return jnp.concatenate([spread, spread], axis=1)


def cross_sums(source, gain, hot, spread, outs):
    slots = outs[0].shape[0]
    each = hot.shape[0] // (len(outs) * slots)
    hidden = jnp.maximum(dot(hot[...], source) + wide(spread[...]) * gain, 0.0)
    for r, out in enumerate(outs):
        total = hidden[r * each * slots : (r * each + 1) * slots]
        for x in range(r * each + 1, (r + 1) * each):
            total = total + hidden[x * slots : (x + 1) * slots]
        out[...] = total.astype(BF16)


def choose(which, refs, rows):
    value = refs[0][rows, :]
    for r in range(1, len(refs)):
        value = jnp.where(which == r, refs[r][rows, :], value)
    return value


def place_of(segment, segments):
    return lax.rem(lax.axis_index("segment") - segment + segments, segments)


def edge_weights(which, j, mine, other, width):
    edge, under = edge_rows(width, j)
    a, b = (choose(which, refs, edge) for refs in (mine, other))
    first = lax.axis_index("chan") == 0
    weights = jnp.concatenate([jnp.where(first, a, b), jnp.where(first, b, a)], axis=0)
    return weights, choose(which, mine, under).astype(F32)


def partner_sums_kernel(segments, *refs):
    mine, other = refs[:segments], refs[segments : 2 * segments]
    raw, outs = refs[2 * segments : 2 * segments + 2], refs[2 * segments + 2 :]
    slots, width = outs[0].shape
    each = (raw[0].shape[0] - VECTORS) // slots
    weights, vectors = edge_weights(place_of(0, segments), 0, mine, other, width)
    for r, out in enumerate(outs):
        block = jnp.where(lax.axis_index("chan") == r, raw[0][...], raw[1][...])
        table = (dot(block[0 : each * slots, :], weights) + vectors[0:1, :]).astype(BF16).astype(F32)
        rows = block[each * slots :, 0:slots].astype(F32)
        coefs = [sum(rows[i : i + 1] for i in range(3 * x + 1, 3 * x + 3)) + rows[3 * x : 3 * x + 1] for x in range(each)]
        coefs = columns(jnp.concatenate(coefs, axis=0))
        total = None
        for x in range(each):
            hidden = table[x * slots : (x + 1) * slots] + coefs[:, x : x + 1] * vectors[1:2, :]
            hidden = jnp.maximum(hidden, 0.0)
            total = hidden if total is None else total + hidden
        out[...] = total.astype(BF16)


def inner_kernel(segments, segment, j, first, *refs):
    mine, other = refs[:segments], refs[segments : 2 * segments]
    source, hot, spread, sums = refs[2 * segments :]
    nodes, width = sums.shape
    which = place_of(segment, segments)
    table = source[...]
    if first:
        weights, vectors = edge_weights(which, j, mine, other, width)
        table = (dot(table, weights) + vectors[0:1, :]).astype(BF16)
    gain = choose(which, mine, edge_rows(width, j)[1]).astype(F32)[1:2, :]
    total = None
    for k in range(hot.shape[0] // nodes):
        rows = pl.ds(k * nodes, nodes)
        hidden = jnp.maximum(dot(hot[rows, :], table) + wide(spread[rows, :]) * gain, 0.0)
        total = hidden if total is None else total + hidden
    sums[...] = total


def weights_kernel(segments, held, segment, j, *refs):
    mine, other, vec_mine, vec_other = (refs[i * segments : (i + 1) * segments] for i in range(4))
    latent, before, chosen = refs[4 * segments :]
    width = before.shape[1]
    half = width // 2
    inner, outer = node_rows(width, held, j)
    which = place_of(segment, segments)
    in_a, in_b = (choose(which, refs, inner) for refs in (mine, other))
    vec_a, vec_b = (choose(which, refs, edge_rows(width, j)[1]) for refs in (vec_mine, vec_other))
    joined = jnp.concatenate([in_a[:, :half], in_b[:, :half]], axis=1)
    bias = jnp.concatenate([vec_a[:, :half], vec_b[:, :half]], axis=1).astype(F32)[4:5, :]
    before[...] = dot(latent[...], joined) + bias
    chosen[0:width, :] = jnp.concatenate([in_a[:, half:], in_b[:, half:]], axis=1)
    for start, refs in ((width, mine), (width + half, other)):
        out = choose(which, refs, outer).astype(F32)
        chosen[start : start + half, :] = (out - jnp.mean(out, axis=1, keepdims=True)).astype(BF16)
    chosen[2 * width : 2 * width + VECTORS, :] = vec_a


def node_kernel(segments, segment, j, last, rounds, *refs):
    arrived, refs = refs[:rounds], refs[rounds:]
    latent, sums, before, chosen, scatter = refs[:5]
    width = sums.shape[1]
    half = width // 2
    nodes = sums.shape[0]
    mine, other = refs[5 : 5 + segments], refs[5 + segments : 5 + 2 * segments]
    if last:
        (result,) = refs[5:]
    else:
        hot, spread, result, source, *outs = refs[5 + 2 * segments :]
        weights, edge_vectors = edge_weights(
            place_of(segment, segments), j, mine, other, width
        )
    blocks = jnp.concatenate([block[...] for block in arrived[::-1]], axis=0)
    vectors = chosen[2 * width : 2 * width + VECTORS, :].astype(F32)
    summed = sums[...] + dot(scatter[...], blocks)
    hidden = before[...] + dot(summed.astype(BF16), chosen[0:width, :])
    hidden = jnp.maximum(hidden, 0.0).astype(BF16)
    centred = dot(hidden, chosen[width : 2 * width, :])
    variance = jnp.mean(centred * centred, axis=1, keepdims=True)
    normed = centred * lax.rsqrt(variance + 1e-05) * vectors[2:3, :] + vectors[3:4, :]
    fresh = (latent[...].astype(F32) + normed).astype(BF16)
    if last:
        result[0] = fresh
        return
    result[...] = fresh
    table = (dot(fresh, weights) + edge_vectors[0:1, :]).astype(BF16)
    source[...] = table
    cross_sums(table, edge_vectors[1:2, :], hot, spread, outs)


def partner_route(count, r):
    return [(i, i ^ 1 << r) for i in range(count) if i ^ 1 << r < count]


def per_device(
    latents,
    neighbors,
    edge_coef,
    cross_src,
    cross_coef,
    recv_node,
    w_edge,
    w_node_in,
    w_node_out,
    edge_bias,
    edge_gain,
    node_bias,
    norm_gain,
    norm_bias,
):
    segments, cores, parts = (lax.axis_size(a) for a in ("segment", "chan", "dom"))
    micro, nodes, width = latents.shape
    held = w_edge.shape[0]
    rounds, slots = recv_node.shape
    degree, edges = neighbors.shape[0], cross_src.shape[0] * cross_src.shape[1]
    half = width // 2
    assert micro == segments and cores == rounds == 2

    def in_hbm(*arrays):
        return [pltpu.with_memory_space_constraint(array, pltpu.HBM) for array in arrays]

    def buffers(*arrays):
        return [pltpu.VMEM(array.shape, array.dtype) for array in arrays]

    def swap(block):
        return lax.ppermute(block, "chan", [(0, 1), (1, 0)])

    def exchange(blocks):
        return [lax.ppermute(block, "dom", partner_route(parts, r)) for r, block in enumerate(blocks)]

    def once(arrays, made):
        return lax.optimization_barrier((arrays, made))[0]

    vectors = (edge_bias, edge_gain, norm_gain, norm_bias, node_bias)
    packs = kernel_call(
        pack_kernel,
        [shape((node_rows(width, held, j)[1].stop, width), BF16) for j in range(held)],
        [*in_hbm(w_edge, w_node_in, w_node_out, *vectors)],
        1 << 10,
        scratch=[*buffers(*vectors), pltpu.SemaphoreType.DMA((5 + 4 * held,))],
    )
    graph = (cross_src, cross_coef, recv_node)
    latent, hot_c, spread_c, scatter, raw = kernel_call(
        cross_prep_kernel,
        [
            shape((nodes, width), BF16),
            shape((edges * slots, nodes), BF16),
            shape((edges * slots, LANES), F32),
            shape((nodes, rounds * slots), BF16),
            shape((edges // rounds * slots + VECTORS, width), BF16),
        ],
        [*in_hbm(latents, *graph), packs[0]],
        1 << 10,
        after=1,
        scratch=[*buffers(*graph), pltpu.SemaphoreType.DMA((4,))],
    )
    route = []
    for core in range(cores):
        route += [(a * cores + core, b * cores + core) for a, b in partner_route(parts, core)]
    raw = lax.ppermute(raw, ("dom", "chan"), route)
    hot, spread = kernel_call(
        inner_prep_kernel,
        [shape((degree * nodes, nodes), BF16), shape((degree * nodes, LANES), F32)],
        [*in_hbm(neighbors, edge_coef), scatter],
        1 << 30,
        after=1,
        scratch=[*buffers(neighbors, edge_coef), pltpu.SemaphoreType.DMA((2,))],
    )
    routes = [[(i, (i + r) % segments) for i in range(segments)] for r in range(1, segments)]
    mine_of, other_of = [], []
    for j in range(held):
        ready = once(packs[j], scatter if j else latents)
        mine_of.append([packs[j], *[lax.ppermute(ready, "segment", route) for route in routes]])

    total = segments * held
    sends = [shape((nodes, width), BF16)] + [shape((slots, width), BF16)] * rounds
    def swaps(j, made):
        return [swap(once(packs[j], scatter)), *map(swap, once(mine_of[j][1:], made))]

    source = latent
    for layer in range(total):
        segment, j = divmod(layer, held)
        if layer == 0:
            other_of.append(swaps(0, (raw, hot)))
        weights = [*mine_of[0], *other_of[0]]
        sums = kernel_call(
            functools.partial(inner_kernel, segments, segment, j, layer == 0),
            shape((nodes, width), F32),
            [*weights, source, hot, spread],
            1 << 31,
        )
        before, chosen = kernel_call(
            functools.partial(weights_kernel, segments, held, segment, j),
            [shape((nodes, width), F32), shape((2 * width + VECTORS, width), BF16)],
            [*mine_of[j], *other_of[j], *weights, latent],
            1 << 28,
        )
        if layer == 0:
            arrived = kernel_call(
                functools.partial(partner_sums_kernel, segments),
                sends[1:],
                [*weights, raw, swap(raw)],
                1 << 28,
            )
        else:
            arrived = exchange(blocks)
        operands = [*arrived[::-1], latent, sums, before, chosen, scatter]
        last = layer == total - 1
        follow, step = divmod(layer + 1, held)
        if last:
            outs = [shape((1, nodes, width), BF16)]
        else:
            operands += [*weights, hot_c, spread_c]
            outs = [shape((nodes, width), BF16), *sends]
        latent, *rest = kernel_call(
            functools.partial(node_kernel, segments, follow, step, last, rounds), outs, operands, 1 << 30
        )
        if not last:
            source, *blocks = rest
        if layer + 1 < held:
            other_of.append(swaps(layer + 1, source))
    return latent


def solution(mesh):
    return jax.shard_map(
        per_device,
        mesh=mesh,
        in_specs=(
            P(None, ("groups", "dom"), None),
            P(None, ("groups", "dom")),
            P(None, ("groups", "dom")),
            P(None, None, ("groups", "dom")),
            P(None, None, ("groups", "dom")),
            P(None, ("groups", "dom")),
            P("segment", None, None),
            P("segment", None, "chan"),
            P("segment", "chan", None),
            P("segment", None),
            P("segment", None),
            P("segment", "chan"),
            P("segment", None),
            P("segment", None),
        ),
        out_specs=P("segment", ("groups", "dom"), None),
        check_vma=False,
    )
```

```python
import functools

import jax
import jax.numpy as jnp
from jax import lax
from jax.experimental import pallas as pl
from jax.experimental.pallas import tpu as pltpu
from jax.sharding import PartitionSpec as P

F32 = jnp.float32
BF16 = jnp.bfloat16
VMEM = pl.BlockSpec(memory_space=pltpu.VMEM)
HBM = pl.BlockSpec(memory_space=pltpu.HBM)
ANY = pl.BlockSpec(memory_space=pl.ANY)
LANES = 128


def dot(a, b):
    return jnp.dot(a, b, preferred_element_type=F32)


def kernel_call(body, outs, operands, flops, scratch=(), after=0):
    plain = len(operands) - after
    return pl.pallas_call(
        body,
        out_shape=outs,
        in_specs=[HBM if scratch else VMEM] * plain + [ANY] * after,
        out_specs=jax.tree.map(lambda _: VMEM, outs),
        scratch_shapes=scratch,
        cost_estimate=pl.CostEstimate(flops=flops, bytes_accessed=1 << 16, transcendentals=0),
        compiler_params=pltpu.CompilerParams(vmem_limit_bytes=24 * 1024 * 1024),
    )(*operands)


def shape(dims, dtype):
    return jax.ShapeDtypeStruct(dims, dtype)


VECTORS = 16


def fetch_all(pairs, sem):
    copies = [pltpu.make_async_copy(a, b, sem.at[i]) for i, (a, b) in enumerate(pairs)]
    for copy in copies:
        copy.start()
    return copies


def vector_rows(rows, width):
    spot = lax.broadcasted_iota(jnp.int32, (VECTORS, width), 0)
    block = jnp.zeros((VECTORS, width), F32)
    for i, row in enumerate(rows):
        row = row.astype(F32)
        if row.shape[1] < width:
            row = jnp.concatenate([row] * (width // row.shape[1]), axis=1)
        block = jnp.where(spot == i, row, block)
    return block.astype(BF16)


def edge_rows(width, j):
    half = width // 2
    start = j * (half + VECTORS)
    return slice(start, start + half), slice(start + half, start + half + VECTORS)


def pack_kernel(w_edge, w_in, w_out, e_bias, e_gain, g_norm, b_norm, n_bias, edge_pack, *refs):
    held, half, width = w_out.shape
    packs, vectors, sem = refs[:held], refs[held:-1], refs[-1]
    mine = pl.multiple_of(lax.axis_index("chan") * half, half)
    pairs = list(zip((e_bias, e_gain, g_norm, b_norm, n_bias), vectors))
    pairs += [(w_edge.at[j, pl.ds(mine, half)], edge_pack.at[edge_rows(width, j)[0]]) for j in range(held)]
    for j in range(held):
        pairs += [
            (w_in.at[j, pl.ds(0, width)], packs[j].at[pl.ds(0, width), pl.ds(0, half)]),
            (w_in.at[j, pl.ds(width, width)], packs[j].at[pl.ds(0, width), pl.ds(half, half)]),
            (w_out.at[j], packs[j].at[pl.ds(width, half)]),
        ]
    copies = fetch_all(pairs, sem)
    for copy in copies[:5]:
        copy.wait()
    for j in range(held):
        edge_pack[edge_rows(width, j)[1], :] = vector_rows([ref[j : j + 1, :] for ref in vectors], width)
    for copy in copies[5:]:
        copy.wait()


def columns(rows):
    rows = rows.astype(F32)
    missing = -rows.shape[0] % 8
    if missing:
        rows = jnp.concatenate([rows, jnp.zeros((missing, rows.shape[1]), F32)], axis=0)
    return rows.T


def one_hot_rows(index_columns, coef_columns, count, nodes, hot, spread):
    rows = index_columns.shape[0]
    lane = lax.broadcasted_iota(jnp.int32, (rows, nodes), 1).astype(F32)
    for k in range(count):
        hot[k * rows : (k + 1) * rows, :] = jnp.where(
            index_columns[:, k : k + 1] == lane, 1.0, 0.0
        ).astype(BF16)
        spread[k * rows : (k + 1) * rows, :] = jnp.broadcast_to(
            coef_columns[:, k : k + 1], (rows, LANES)
        )


def pieces(values):
    high = values.astype(BF16)
    rest = values - high.astype(F32)
    middle = rest.astype(BF16)
    return high, middle, (rest - middle.astype(F32)).astype(BF16)


def cross_prep_kernel(latents, src, coef, recv, _, latent, hot, spread, scatter, *refs):
    rounds, slots = recv.shape
    raw, here, sem = refs[0], refs[1:4], refs[4]
    copies = fetch_all([*zip((src, coef, recv), here), (latents.at[lax.axis_index("segment")], latent)], sem)
    for copy in copies[:3]:
        copy.wait()
    nodes, width = latent.shape
    whole = [jnp.concatenate([ref[r] for r in range(rounds)], axis=0) for ref in here[:2]]
    one_hot_rows(columns(whole[0]), columns(whole[1]), whole[0].shape[0], nodes, hot, spread)
    row = lax.broadcasted_iota(jnp.int32, (nodes, slots), 0)
    for r in range(rounds):
        scatter[:, r * slots : (r + 1) * slots] = jnp.where(
            here[2][r : r + 1, :] == row, 1.0, 0.0
        ).astype(BF16)
    copies[3].wait()
    each = src.shape[1] * slots
    mine = pl.multiple_of(lax.axis_index("chan") * each, each)
    raw[0:each, :] = dot(hot[pl.ds(mine, each), :], latent[...]).astype(BF16)
    coefs = here[1][lax.axis_index("chan")]
    rows = [piece[x : x + 1, :] for x in range(src.shape[1]) for piece in pieces(coefs)]
    raw[each : each + VECTORS, :] = vector_rows(rows, width)


def inner_prep_kernel(neighbors, coef, _, hot, spread, neighbors_here, coef_here, sem):
    for copy in fetch_all([(neighbors, neighbors_here), (coef, coef_here)], sem):
        copy.wait()
    degree, nodes = neighbors.shape
    one_hot_rows(columns(neighbors_here[...]), columns(coef_here[...]), degree, nodes, hot, spread)


def wide(spread):
    return jnp.concatenate([spread, spread], axis=1)


def cross_sums(source, gain, hot, spread, outs):
    slots = outs[0].shape[0]
    each = hot.shape[0] // (len(outs) * slots)
    hidden = jnp.maximum(dot(hot[...], source) + wide(spread[...]) * gain, 0.0)
    for r, out in enumerate(outs):
        total = hidden[r * each * slots : (r * each + 1) * slots]
        for x in range(r * each + 1, (r + 1) * each):
            total = total + hidden[x * slots : (x + 1) * slots]
        out[...] = total.astype(BF16)


def choose(which, refs, rows):
    value = refs[0][rows, :]
    for r in range(1, len(refs)):
        value = jnp.where(which == r, refs[r][rows, :], value)
    return value


def place_of(segment, segments):
    return lax.rem(lax.axis_index("segment") - segment + segments, segments)


def edge_weights(which, j, mine, other, width):
    edge, under = edge_rows(width, j)
    a, b = (choose(which, refs, edge) for refs in (mine, other))
    first = lax.axis_index("chan") == 0
    weights = jnp.concatenate([jnp.where(first, a, b), jnp.where(first, b, a)], axis=0)
    return weights, choose(which, mine, under).astype(F32)


def partner_sums_kernel(segments, *refs):
    mine, other = refs[:segments], refs[segments : 2 * segments]
    raw, outs = refs[2 * segments : 2 * segments + 2], refs[2 * segments + 2 :]
    slots, width = outs[0].shape
    each = (raw[0].shape[0] - VECTORS) // slots
    weights, vectors = edge_weights(place_of(0, segments), 0, mine, other, width)
    for r, out in enumerate(outs):
        block = jnp.where(lax.axis_index("chan") == r, raw[0][...], raw[1][...])
        table = (dot(block[0 : each * slots, :], weights) + vectors[0:1, :]).astype(BF16).astype(F32)
        rows = block[each * slots :, 0:slots].astype(F32)
        coefs = [sum(rows[i : i + 1] for i in range(3 * x + 1, 3 * x + 3)) + rows[3 * x : 3 * x + 1] for x in range(each)]
        coefs = columns(jnp.concatenate(coefs, axis=0))
        total = None
        for x in range(each):
            hidden = table[x * slots : (x + 1) * slots] + coefs[:, x : x + 1] * vectors[1:2, :]
            hidden = jnp.maximum(hidden, 0.0)
            total = hidden if total is None else total + hidden
        out[...] = total.astype(BF16)


def inner_kernel(segments, segment, j, first, *refs):
    mine, other = refs[:segments], refs[segments : 2 * segments]
    source, hot, spread, *_, sums = refs[2 * segments :]
    nodes, width = sums.shape
    which = place_of(segment, segments)
    table = source[...]
    if first:
        weights, vectors = edge_weights(which, j, mine, other, width)
        table = (dot(table, weights) + vectors[0:1, :]).astype(BF16)
    gain = choose(which, mine, edge_rows(width, j)[1]).astype(F32)[1:2, :]
    total = None
    for k in range(hot.shape[0] // nodes):
        rows = pl.ds(k * nodes, nodes)
        hidden = jnp.maximum(dot(hot[rows, :], table) + wide(spread[rows, :]) * gain, 0.0)
        total = hidden if total is None else total + hidden
    sums[...] = total


def weights_kernel(segments, segment, j, *refs):
    mine, other, vec_mine, vec_other = (refs[i * segments : (i + 1) * segments] for i in range(4))
    latent, before, chosen = refs[4 * segments :]
    width = before.shape[1]
    half = width // 2
    inner, outer = slice(0, width), slice(width, width + half)
    which = place_of(segment, segments)
    in_a, in_b = (choose(which, refs, inner) for refs in (mine, other))
    vec_a, vec_b = (choose(which, refs, edge_rows(width, j)[1]) for refs in (vec_mine, vec_other))
    joined = jnp.concatenate([in_a[:, :half], in_b[:, :half]], axis=1)
    bias = jnp.concatenate([vec_a[:, :half], vec_b[:, :half]], axis=1).astype(F32)[4:5, :]
    before[...] = dot(latent[...], joined) + bias
    chosen[0:width, :] = jnp.concatenate([in_a[:, half:], in_b[:, half:]], axis=1)
    for start, refs in ((width, mine), (width + half, other)):
        out = choose(which, refs, outer).astype(F32)
        chosen[start : start + half, :] = (out - jnp.mean(out, axis=1, keepdims=True)).astype(BF16)
    chosen[2 * width : 2 * width + VECTORS, :] = vec_a


def node_kernel(segments, segment, j, last, rounds, *refs):
    arrived, refs = refs[:rounds], refs[rounds:]
    latent, sums, before, chosen, scatter = refs[:5]
    width = sums.shape[1]
    half = width // 2
    nodes = sums.shape[0]
    mine, other = refs[5 : 5 + segments], refs[5 + segments : 5 + 2 * segments]
    if last:
        (result,) = refs[5:]
    else:
        hot, spread, result, source, *outs = refs[5 + 2 * segments :]
        weights, edge_vectors = edge_weights(
            place_of(segment, segments), j, mine, other, width
        )
    blocks = jnp.concatenate([block[...] for block in arrived[::-1]], axis=0)
    vectors = chosen[2 * width : 2 * width + VECTORS, :].astype(F32)
    summed = sums[...] + dot(scatter[...], blocks)
    hidden = before[...] + dot(summed.astype(BF16), chosen[0:width, :])
    hidden = jnp.maximum(hidden, 0.0).astype(BF16)
    centred = dot(hidden, chosen[width : 2 * width, :])
    variance = jnp.mean(centred * centred, axis=1, keepdims=True)
    normed = centred * lax.rsqrt(variance + 1e-05) * vectors[2:3, :] + vectors[3:4, :]
    fresh = (latent[...].astype(F32) + normed).astype(BF16)
    if last:
        result[0] = fresh
        return
    result[...] = fresh
    table = (dot(fresh, weights) + edge_vectors[0:1, :]).astype(BF16)
    source[...] = table
    cross_sums(table, edge_vectors[1:2, :], hot, spread, outs)


def partner_route(count, r):
    return [(i, i ^ 1 << r) for i in range(count) if i ^ 1 << r < count]


def per_device(
    latents,
    neighbors,
    edge_coef,
    cross_src,
    cross_coef,
    recv_node,
    w_edge,
    w_node_in,
    w_node_out,
    edge_bias,
    edge_gain,
    node_bias,
    norm_gain,
    norm_bias,
):
    segments, cores, parts = (lax.axis_size(a) for a in ("segment", "chan", "dom"))
    micro, nodes, width = latents.shape
    held = w_edge.shape[0]
    rounds, slots = recv_node.shape
    degree, edges = neighbors.shape[0], cross_src.shape[0] * cross_src.shape[1]
    half = width // 2
    assert micro == segments and cores == rounds == 2

    def in_hbm(*arrays):
        return [pltpu.with_memory_space_constraint(array, pltpu.HBM) for array in arrays]

    def buffers(*arrays):
        return [pltpu.VMEM(array.shape, array.dtype) for array in arrays]

    def swap(block):
        return lax.ppermute(block, "chan", [(0, 1), (1, 0)])

    def exchange(blocks):
        return [lax.ppermute(block, "dom", partner_route(parts, r)) for r, block in enumerate(blocks)]

    def once(arrays, made):
        return lax.optimization_barrier((arrays, made))[0]

    vectors = (edge_bias, edge_gain, norm_gain, norm_bias, node_bias)
    edge_pack, *node_packs = kernel_call(
        pack_kernel,
        [shape((edge_rows(width, held)[0].start, width), BF16)] + [shape((width + half, width), BF16)] * held,
        [*in_hbm(w_edge, w_node_in, w_node_out, *vectors)],
        1 << 10,
        scratch=[*buffers(*vectors), pltpu.SemaphoreType.DMA((5 + 4 * held,))],
    )
    graph = (cross_src, cross_coef, recv_node)
    latent, hot_c, spread_c, scatter, raw = kernel_call(
        cross_prep_kernel,
        [
            shape((nodes, width), BF16),
            shape((edges * slots, nodes), BF16),
            shape((edges * slots, LANES), F32),
            shape((nodes, rounds * slots), BF16),
            shape((edges // rounds * slots + VECTORS, width), BF16),
        ],
        [*in_hbm(latents, *graph), edge_pack],
        1 << 10,
        after=1,
        scratch=[*buffers(*graph), pltpu.SemaphoreType.DMA((4,))],
    )
    route = []
    for core in range(cores):
        route += [(a * cores + core, b * cores + core) for a, b in partner_route(parts, core)]
    raw = lax.ppermute(raw, ("dom", "chan"), route)
    hot, spread = kernel_call(
        inner_prep_kernel,
        [shape((degree * nodes, nodes), BF16), shape((degree * nodes, LANES), F32)],
        [*in_hbm(neighbors, edge_coef), scatter],
        1 << 30,
        after=1,
        scratch=[*buffers(neighbors, edge_coef), pltpu.SemaphoreType.DMA((2,))],
    )
    routes = [[(i, (i + r) % segments) for i in range(segments)] for r in range(1, segments)]

    def spread_out(pack):
        return [lax.ppermute(pack, "segment", route) for route in routes]

    edges_mine = spread_out(edge_pack)
    nodes_mine = [spread_out(once(pack, scatter) if j else pack) for j, pack in enumerate(node_packs)]

    def swaps(own, received, made):
        return [own, *received, swap(once(own, scatter)), *map(swap, once(received, made))]

    weights = swaps(edge_pack, edges_mine, (raw, hot))
    node_weights = [None] * held
    node_weights[0] = swaps(node_packs[0], nodes_mine[0], weights[-1])
    total = segments * held
    sends = [shape((nodes, width), BF16)] + [shape((slots, width), BF16)] * rounds
    source = latent
    for layer in range(total):
        segment, j = divmod(layer, held)
        sums = kernel_call(
            functools.partial(inner_kernel, segments, segment, j, layer == 0),
            shape((nodes, width), F32),
            [*weights, source, hot, spread, *(() if layer else nodes_mine[0])],
            1 << 31,
            after=0 if layer else segments - 1,
        )
        if layer == 0:
            arrived = kernel_call(
                functools.partial(partner_sums_kernel, segments),
                sends[1:],
                [*weights, raw, swap(raw)],
                1 << 28,
            )
        else:
            arrived = exchange(blocks)
        if 0 < layer < held:
            node_weights[j] = swaps(node_packs[j], nodes_mine[j], arrived[0])
        before, chosen = kernel_call(
            functools.partial(weights_kernel, segments, segment, j),
            [shape((nodes, width), F32), shape((2 * width + VECTORS, width), BF16)],
            [*node_weights[j], *weights, latent],
            1 << 28,
        )
        operands = [*arrived[::-1], latent, sums, before, chosen, scatter]
        last = layer == total - 1
        follow, step = divmod(layer + 1, held)
        if last:
            outs = [shape((1, nodes, width), BF16)]
        else:
            operands += [*weights, hot_c, spread_c]
            outs = [shape((nodes, width), BF16), *sends]
        latent, *rest = kernel_call(
            functools.partial(node_kernel, segments, follow, step, last, rounds), outs, operands, 1 << 30
        )
        if not last:
            source, *blocks = rest
    return latent


def solution(mesh):
    return jax.shard_map(
        per_device,
        mesh=mesh,
        in_specs=(
            P(None, ("groups", "dom"), None),
            P(None, ("groups", "dom")),
            P(None, ("groups", "dom")),
            P(None, None, ("groups", "dom")),
            P(None, None, ("groups", "dom")),
            P(None, ("groups", "dom")),
            P("segment", None, None),
            P("segment", None, "chan"),
            P("segment", "chan", None),
            P("segment", None),
            P("segment", None),
            P("segment", "chan"),
            P("segment", None),
            P("segment", None),
        ),
        out_specs=P("segment", ("groups", "dom"), None),
        check_vma=False,
    )
```

```python
import functools

import jax
import jax.numpy as jnp
from jax import lax
from jax.experimental import pallas as pl
from jax.experimental.pallas import tpu as pltpu
from jax.sharding import PartitionSpec as P

F32 = jnp.float32
BF16 = jnp.bfloat16
VMEM = pl.BlockSpec(memory_space=pltpu.VMEM)
HBM = pl.BlockSpec(memory_space=pltpu.HBM)
ANY = pl.BlockSpec(memory_space=pl.ANY)
LANES = 128


def dot(a, b):
    return jnp.dot(a, b, preferred_element_type=F32)


def kernel_call(body, outs, operands, flops, scratch=(), after=0):
    plain = len(operands) - after
    return pl.pallas_call(
        body,
        out_shape=outs,
        in_specs=[HBM if scratch else VMEM] * plain + [ANY] * after,
        out_specs=jax.tree.map(lambda _: VMEM, outs),
        scratch_shapes=scratch,
        cost_estimate=pl.CostEstimate(flops=flops, bytes_accessed=1 << 16, transcendentals=0),
        compiler_params=pltpu.CompilerParams(vmem_limit_bytes=24 * 1024 * 1024),
    )(*operands)


def shape(dims, dtype):
    return jax.ShapeDtypeStruct(dims, dtype)


VECTORS = 16


def fetch_all(pairs, sem):
    copies = [pltpu.make_async_copy(a, b, sem.at[i]) for i, (a, b) in enumerate(pairs)]
    for copy in copies:
        copy.start()
    return copies


def vector_rows(rows, width):
    spot = lax.broadcasted_iota(jnp.int32, (VECTORS, width), 0)
    block = jnp.zeros((VECTORS, width), F32)
    for i, row in enumerate(rows):
        row = row.astype(F32)
        if row.shape[1] < width:
            row = jnp.concatenate([row] * (width // row.shape[1]), axis=1)
        block = jnp.where(spot == i, row, block)
    return block.astype(BF16)


def edge_rows(width, j):
    half = width // 2
    start = j * (half + VECTORS)
    return slice(start, start + half), slice(start + half, start + half + VECTORS)


def pack_kernel(w_edge, w_in, w_out, e_bias, e_gain, g_norm, b_norm, n_bias, edge_pack, *refs):
    held, half, width = w_out.shape
    packs, vectors, sem = refs[:held], refs[held:-1], refs[-1]
    mine = pl.multiple_of(lax.axis_index("chan") * half, half)
    pairs = list(zip((e_bias, e_gain, g_norm, b_norm, n_bias), vectors))
    pairs += [(w_edge.at[j, pl.ds(mine, half)], edge_pack.at[edge_rows(width, j)[0]]) for j in range(held)]
    for j in range(held):
        pairs += [
            (w_in.at[j, pl.ds(0, width)], packs[j].at[pl.ds(0, width), pl.ds(0, half)]),
            (w_in.at[j, pl.ds(width, width)], packs[j].at[pl.ds(0, width), pl.ds(half, half)]),
            (w_out.at[j], packs[j].at[pl.ds(width, half)]),
        ]
    copies = fetch_all(pairs, sem)
    for copy in copies[:5]:
        copy.wait()
    for j in range(held):
        edge_pack[edge_rows(width, j)[1], :] = vector_rows([ref[j : j + 1, :] for ref in vectors], width)
    for copy in copies[5:]:
        copy.wait()


def columns(rows):
    rows = rows.astype(F32)
    missing = -rows.shape[0] % 8
    if missing:
        rows = jnp.concatenate([rows, jnp.zeros((missing, rows.shape[1]), F32)], axis=0)
    return rows.T


def one_hot_rows(index_columns, coef_columns, count, nodes, hot, spread):
    rows = index_columns.shape[0]
    lane = lax.broadcasted_iota(jnp.int32, (rows, nodes), 1).astype(F32)
    for k in range(count):
        hot[k * rows : (k + 1) * rows, :] = jnp.where(
            index_columns[:, k : k + 1] == lane, 1.0, 0.0
        ).astype(BF16)
        spread[k * rows : (k + 1) * rows, :] = jnp.broadcast_to(
            coef_columns[:, k : k + 1], (rows, LANES)
        )


def pieces(values):
    high = values.astype(BF16)
    rest = values - high.astype(F32)
    middle = rest.astype(BF16)
    return high, middle, (rest - middle.astype(F32)).astype(BF16)


def cross_prep_kernel(latents, src, coef, recv, _, latent, hot, spread, scatter, *refs):
    rounds, slots = recv.shape
    raw, here, sem = refs[0], refs[1:4], refs[4]
    copies = fetch_all([*zip((src, coef, recv), here), (latents.at[lax.axis_index("segment")], latent)], sem)
    for copy in copies[:3]:
        copy.wait()
    nodes, width = latent.shape
    whole = [jnp.concatenate([ref[r] for r in range(rounds)], axis=0) for ref in here[:2]]
    one_hot_rows(columns(whole[0]), columns(whole[1]), whole[0].shape[0], nodes, hot, spread)
    row = lax.broadcasted_iota(jnp.int32, (nodes, slots), 0)
    for r in range(rounds):
        scatter[:, r * slots : (r + 1) * slots] = jnp.where(
            here[2][r : r + 1, :] == row, 1.0, 0.0
        ).astype(BF16)
    copies[3].wait()
    each = src.shape[1] * slots
    mine = pl.multiple_of(lax.axis_index("chan") * each, each)
    raw[0:each, :] = dot(hot[pl.ds(mine, each), :], latent[...]).astype(BF16)
    coefs = here[1][lax.axis_index("chan")]
    rows = [piece[x : x + 1, :] for x in range(src.shape[1]) for piece in pieces(coefs)]
    raw[each : each + VECTORS, :] = vector_rows(rows, width)


def inner_prep_kernel(neighbors, coef, _, hot, spread, neighbors_here, coef_here, sem):
    for copy in fetch_all([(neighbors, neighbors_here), (coef, coef_here)], sem):
        copy.wait()
    degree, nodes = neighbors.shape
    one_hot_rows(columns(neighbors_here[...]), columns(coef_here[...]), degree, nodes, hot, spread)


def wide(spread):
    return jnp.concatenate([spread, spread], axis=1)


def cross_sums(source, gain, hot, spread, outs):
    slots = outs[0].shape[0]
    each = hot.shape[0] // (len(outs) * slots)
    hidden = jnp.maximum(dot(hot[...], source) + wide(spread[...]) * gain, 0.0)
    for r, out in enumerate(outs):
        total = hidden[r * each * slots : (r * each + 1) * slots]
        for x in range(r * each + 1, (r + 1) * each):
            total = total + hidden[x * slots : (x + 1) * slots]
        out[...] = total.astype(BF16)


def choose(which, refs, rows):
    value = refs[0][rows, :]
    for r in range(1, len(refs)):
        value = jnp.where(which == r, refs[r][rows, :], value)
    return value


def place_of(segment, segments):
    return lax.rem(lax.axis_index("segment") - segment + segments, segments)


def edge_weights(which, j, mine, other, width):
    edge, under = edge_rows(width, j)
    a, b = (choose(which, refs, edge) for refs in (mine, other))
    first = lax.axis_index("chan") == 0
    weights = jnp.concatenate([jnp.where(first, a, b), jnp.where(first, b, a)], axis=0)
    return weights, choose(which, mine, under).astype(F32)


def partner_sums_kernel(segments, *refs):
    mine, other = refs[:segments], refs[segments : 2 * segments]
    raw, outs = refs[2 * segments : 2 * segments + 2], refs[2 * segments + 2 :]
    slots, width = outs[0].shape
    each = (raw[0].shape[0] - VECTORS) // slots
    weights, vectors = edge_weights(place_of(0, segments), 0, mine, other, width)
    for r, out in enumerate(outs):
        block = jnp.where(lax.axis_index("chan") == r, raw[0][...], raw[1][...])
        table = (dot(block[0 : each * slots, :], weights) + vectors[0:1, :]).astype(BF16).astype(F32)
        rows = block[each * slots :, 0:slots].astype(F32)
        coefs = [sum(rows[i : i + 1] for i in range(3 * x + 1, 3 * x + 3)) + rows[3 * x : 3 * x + 1] for x in range(each)]
        coefs = columns(jnp.concatenate(coefs, axis=0))
        total = None
        for x in range(each):
            hidden = table[x * slots : (x + 1) * slots] + coefs[:, x : x + 1] * vectors[1:2, :]
            hidden = jnp.maximum(hidden, 0.0)
            total = hidden if total is None else total + hidden
        out[...] = total.astype(BF16)


def inner_kernel(segments, segment, j, first, *refs):
    mine, other = refs[:segments], refs[segments : 2 * segments]
    source, hot, spread, *_, sums = refs[2 * segments :]
    nodes, width = sums.shape
    which = place_of(segment, segments)
    table = source[...]
    if first:
        weights, vectors = edge_weights(which, j, mine, other, width)
        table = (dot(table, weights) + vectors[0:1, :]).astype(BF16)
    gain = choose(which, mine, edge_rows(width, j)[1]).astype(F32)[1:2, :]
    total = None
    for k in range(hot.shape[0] // nodes):
        rows = pl.ds(k * nodes, nodes)
        hidden = jnp.maximum(dot(hot[rows, :], table) + wide(spread[rows, :]) * gain, 0.0)
        total = hidden if total is None else total + hidden
    sums[...] = total


def weights_kernel(segments, segment, j, *refs):
    mine, other, vec_mine, vec_other = (refs[i * segments : (i + 1) * segments] for i in range(4))
    latent, before, chosen = refs[4 * segments :]
    width = before.shape[1]
    half = width // 2
    inner, outer = slice(0, width), slice(width, width + half)
    which = place_of(segment, segments)
    in_a, in_b = (choose(which, refs, inner) for refs in (mine, other))
    vec_a, vec_b = (choose(which, refs, edge_rows(width, j)[1]) for refs in (vec_mine, vec_other))
    joined = jnp.concatenate([in_a[:, :half], in_b[:, :half]], axis=1)
    bias = jnp.concatenate([vec_a[:, :half], vec_b[:, :half]], axis=1).astype(F32)[4:5, :]
    before[...] = dot(latent[...], joined) + bias
    chosen[0:width, :] = jnp.concatenate([in_a[:, half:], in_b[:, half:]], axis=1)
    for start, refs in ((width, mine), (width + half, other)):
        out = choose(which, refs, outer).astype(F32)
        chosen[start : start + half, :] = (out - jnp.mean(out, axis=1, keepdims=True)).astype(BF16)
    chosen[2 * width : 2 * width + VECTORS, :] = vec_a


def node_kernel(segments, segment, j, last, rounds, *refs):
    arrived, refs = refs[:rounds], refs[rounds:]
    latent, sums, before, chosen, scatter = refs[:5]
    width = sums.shape[1]
    half = width // 2
    nodes = sums.shape[0]
    mine, other = refs[5 : 5 + segments], refs[5 + segments : 5 + 2 * segments]
    if last:
        (result,) = refs[5:]
    else:
        hot, spread, result, source, *outs = refs[5 + 2 * segments :]
        weights, edge_vectors = edge_weights(
            place_of(segment, segments), j, mine, other, width
        )
    blocks = jnp.concatenate([block[...] for block in arrived[::-1]], axis=0)
    vectors = chosen[2 * width : 2 * width + VECTORS, :].astype(F32)
    summed = sums[...] + dot(scatter[...], blocks)
    hidden = before[...] + dot(summed.astype(BF16), chosen[0:width, :])
    hidden = jnp.maximum(hidden, 0.0).astype(BF16)
    centred = dot(hidden, chosen[width : 2 * width, :])
    variance = jnp.mean(centred * centred, axis=1, keepdims=True)
    normed = centred * lax.rsqrt(variance + 1e-05) * vectors[2:3, :] + vectors[3:4, :]
    fresh = (latent[...].astype(F32) + normed).astype(BF16)
    if last:
        result[0] = fresh
        return
    result[...] = fresh
    table = (dot(fresh, weights) + edge_vectors[0:1, :]).astype(BF16)
    source[...] = table
    cross_sums(table, edge_vectors[1:2, :], hot, spread, outs)


def partner_route(count, r):
    return [(i, i ^ 1 << r) for i in range(count) if i ^ 1 << r < count]


def per_device(
    latents,
    neighbors,
    edge_coef,
    cross_src,
    cross_coef,
    recv_node,
    w_edge,
    w_node_in,
    w_node_out,
    edge_bias,
    edge_gain,
    node_bias,
    norm_gain,
    norm_bias,
):
    segments, cores, parts = (lax.axis_size(a) for a in ("segment", "chan", "dom"))
    micro, nodes, width = latents.shape
    held = w_edge.shape[0]
    rounds, slots = recv_node.shape
    degree, edges = neighbors.shape[0], cross_src.shape[0] * cross_src.shape[1]
    half = width // 2
    assert micro == segments and cores == rounds == 2

    def in_hbm(*arrays):
        return [pltpu.with_memory_space_constraint(array, pltpu.HBM) for array in arrays]

    def buffers(*arrays):
        return [pltpu.VMEM(array.shape, array.dtype) for array in arrays]

    def swap(block):
        return lax.ppermute(block, "chan", [(0, 1), (1, 0)])

    def exchange(blocks):
        return [lax.ppermute(block, "dom", partner_route(parts, r)) for r, block in enumerate(blocks)]

    def once(arrays, made):
        return lax.optimization_barrier((arrays, made))[0]

    vectors = (edge_bias, edge_gain, norm_gain, norm_bias, node_bias)
    edge_pack, *node_packs = kernel_call(
        pack_kernel,
        [shape((edge_rows(width, held)[0].start, width), BF16)] + [shape((width + half, width), BF16)] * held,
        [*in_hbm(w_edge, w_node_in, w_node_out, *vectors)],
        1 << 10,
        scratch=[*buffers(*vectors), pltpu.SemaphoreType.DMA((5 + 4 * held,))],
    )
    graph = (cross_src, cross_coef, recv_node)
    latent, hot_c, spread_c, scatter, raw = kernel_call(
        cross_prep_kernel,
        [
            shape((nodes, width), BF16),
            shape((edges * slots, nodes), BF16),
            shape((edges * slots, LANES), F32),
            shape((nodes, rounds * slots), BF16),
            shape((edges // rounds * slots + VECTORS, width), BF16),
        ],
        [*in_hbm(latents, *graph), edge_pack],
        1 << 10,
        after=1,
        scratch=[*buffers(*graph), pltpu.SemaphoreType.DMA((4,))],
    )
    route = []
    for core in range(cores):
        route += [(a * cores + core, b * cores + core) for a, b in partner_route(parts, core)]
    raw = lax.ppermute(raw, ("dom", "chan"), route)
    hot, spread = kernel_call(
        inner_prep_kernel,
        [shape((degree * nodes, nodes), BF16), shape((degree * nodes, LANES), F32)],
        [*in_hbm(neighbors, edge_coef), scatter],
        1 << 30,
        after=1,
        scratch=[*buffers(neighbors, edge_coef), pltpu.SemaphoreType.DMA((2,))],
    )
    routes = [[(i, (i + r) % segments) for i in range(segments)] for r in range(1, segments)]

    def spread_out(pack):
        return [lax.ppermute(pack, "segment", route) for route in routes]

    edges_mine = spread_out(edge_pack)
    nodes_mine = [spread_out(once(pack, scatter) if j else pack) for j, pack in enumerate(node_packs)]

    def swaps(own, received, made):
        return [own, *received, swap(once(own, scatter)), *map(swap, once(received, made))]

    def crossed(pack):
        return [
            lax.ppermute(
                pack,
                ("segment", "chan"),
                [(a * cores + core, b * cores + 1 - core) for a, b in route for core in range(cores)],
            )
            for route in routes
        ]

    weights = swaps(edge_pack, edges_mine, (raw, hot))
    node_weights = [None] * held
    node_weights[0] = swaps(node_packs[0], nodes_mine[0], weights[-1])
    for j in range(1, held):
        pack = once(node_packs[j], scatter)
        node_weights[j] = [node_packs[j], *nodes_mine[j], swap(pack), *crossed(pack)]
    total = segments * held
    sends = [shape((nodes, width), BF16)] + [shape((slots, width), BF16)] * rounds
    source = latent
    for layer in range(total):
        segment, j = divmod(layer, held)
        sums = kernel_call(
            functools.partial(inner_kernel, segments, segment, j, layer == 0),
            shape((nodes, width), F32),
            [*weights, source, hot, spread, *(() if layer else nodes_mine[0])],
            1 << 31,
            after=0 if layer else segments - 1,
        )
        if layer == 0:
            arrived = kernel_call(
                functools.partial(partner_sums_kernel, segments),
                sends[1:],
                [*weights, raw, swap(raw)],
                1 << 28,
            )
        else:
            arrived = exchange(blocks)
        before, chosen = kernel_call(
            functools.partial(weights_kernel, segments, segment, j),
            [shape((nodes, width), F32), shape((2 * width + VECTORS, width), BF16)],
            [*node_weights[j], *weights, latent],
            1 << 28,
        )
        operands = [*arrived[::-1], latent, sums, before, chosen, scatter]
        last = layer == total - 1
        follow, step = divmod(layer + 1, held)
        if last:
            outs = [shape((1, nodes, width), BF16)]
        else:
            operands += [*weights, hot_c, spread_c]
            outs = [shape((nodes, width), BF16), *sends]
        latent, *rest = kernel_call(
            functools.partial(node_kernel, segments, follow, step, last, rounds), outs, operands, 1 << 30
        )
        if not last:
            source, *blocks = rest
    return latent


def solution(mesh):
    return jax.shard_map(
        per_device,
        mesh=mesh,
        in_specs=(
            P(None, ("groups", "dom"), None),
            P(None, ("groups", "dom")),
            P(None, ("groups", "dom")),
            P(None, None, ("groups", "dom")),
            P(None, None, ("groups", "dom")),
            P(None, ("groups", "dom")),
            P("segment", None, None),
            P("segment", None, "chan"),
            P("segment", "chan", None),
            P("segment", None),
            P("segment", None),
            P("segment", "chan"),
            P("segment", None),
            P("segment", None),
        ),
        out_specs=P("segment", ("groups", "dom"), None),
        check_vma=False,
    )
```

```python
import functools

import jax
import jax.numpy as jnp
from jax import lax
from jax.experimental import pallas as pl
from jax.experimental.pallas import tpu as pltpu
from jax.sharding import PartitionSpec as P

F32 = jnp.float32
BF16 = jnp.bfloat16
VMEM = pl.BlockSpec(memory_space=pltpu.VMEM)
HBM = pl.BlockSpec(memory_space=pltpu.HBM)
ANY = pl.BlockSpec(memory_space=pl.ANY)
LANES = 128


def dot(a, b):
    return jnp.dot(a, b, preferred_element_type=F32)


def kernel_call(body, outs, operands, flops, scratch=(), after=0):
    plain = len(operands) - after
    return pl.pallas_call(
        body,
        out_shape=outs,
        in_specs=[HBM if scratch else VMEM] * plain + [ANY] * after,
        out_specs=jax.tree.map(lambda _: VMEM, outs),
        scratch_shapes=scratch,
        cost_estimate=pl.CostEstimate(flops=flops, bytes_accessed=1 << 16, transcendentals=0),
        compiler_params=pltpu.CompilerParams(vmem_limit_bytes=24 * 1024 * 1024),
    )(*operands)


def shape(dims, dtype):
    return jax.ShapeDtypeStruct(dims, dtype)


VECTORS = 16


def fetch_all(pairs, sem):
    copies = [pltpu.make_async_copy(a, b, sem.at[i]) for i, (a, b) in enumerate(pairs)]
    for copy in copies:
        copy.start()
    return copies


def vector_rows(rows, width):
    spot = lax.broadcasted_iota(jnp.int32, (VECTORS, width), 0)
    block = jnp.zeros((VECTORS, width), F32)
    for i, row in enumerate(rows):
        row = row.astype(F32)
        if row.shape[1] < width:
            row = jnp.concatenate([row] * (width // row.shape[1]), axis=1)
        block = jnp.where(spot == i, row, block)
    return block.astype(BF16)


def edge_rows(width, j):
    half = width // 2
    start = j * (half + VECTORS)
    return slice(start, start + half), slice(start + half, start + half + VECTORS)


def pack_kernel(w_edge, w_in, w_out, e_bias, e_gain, g_norm, b_norm, n_bias, edge_pack, *refs):
    held, half, width = w_out.shape
    packs, vectors, sem = refs[:held], refs[held:-1], refs[-1]
    mine = pl.multiple_of(lax.axis_index("chan") * half, half)
    pairs = list(zip((e_bias, e_gain, g_norm, b_norm, n_bias), vectors))
    pairs += [(w_edge.at[j, pl.ds(mine, half)], edge_pack.at[edge_rows(width, j)[0]]) for j in range(held)]
    for j in range(held):
        pairs += [
            (w_in.at[j, pl.ds(0, width)], packs[j].at[pl.ds(0, width), pl.ds(0, half)]),
            (w_in.at[j, pl.ds(width, width)], packs[j].at[pl.ds(0, width), pl.ds(half, half)]),
            (w_out.at[j], packs[j].at[pl.ds(width, half)]),
        ]
    copies = fetch_all(pairs, sem)
    for copy in copies[:5]:
        copy.wait()
    for j in range(held):
        edge_pack[edge_rows(width, j)[1], :] = vector_rows([ref[j : j + 1, :] for ref in vectors], width)
    for copy in copies[5:]:
        copy.wait()


def columns(rows):
    rows = rows.astype(F32)
    missing = -rows.shape[0] % 8
    if missing:
        rows = jnp.concatenate([rows, jnp.zeros((missing, rows.shape[1]), F32)], axis=0)
    return rows.T


def one_hot_rows(index_columns, coef_columns, count, nodes, hot, spread):
    rows = index_columns.shape[0]
    lane = lax.broadcasted_iota(jnp.int32, (rows, nodes), 1).astype(F32)
    for k in range(count):
        hot[k * rows : (k + 1) * rows, :] = jnp.where(
            index_columns[:, k : k + 1] == lane, 1.0, 0.0
        ).astype(BF16)
        spread[k * rows : (k + 1) * rows, :] = jnp.broadcast_to(
            coef_columns[:, k : k + 1], (rows, LANES)
        )


def pieces(values):
    high = values.astype(BF16)
    rest = values - high.astype(F32)
    middle = rest.astype(BF16)
    return high, middle, (rest - middle.astype(F32)).astype(BF16)


def cross_prep_kernel(latents, src, coef, recv, _, latent, hot, spread, scatter, *refs):
    rounds, slots = recv.shape
    raw, here, sem = refs[0], refs[1:4], refs[4]
    copies = fetch_all([*zip((src, coef, recv), here), (latents.at[lax.axis_index("segment")], latent)], sem)
    for copy in copies[:3]:
        copy.wait()
    nodes, width = latent.shape
    whole = [jnp.concatenate([ref[r] for r in range(rounds)], axis=0) for ref in here[:2]]
    one_hot_rows(columns(whole[0]), columns(whole[1]), whole[0].shape[0], nodes, hot, spread)
    row = lax.broadcasted_iota(jnp.int32, (nodes, slots), 0)
    for r in range(rounds):
        scatter[:, r * slots : (r + 1) * slots] = jnp.where(
            here[2][r : r + 1, :] == row, 1.0, 0.0
        ).astype(BF16)
    copies[3].wait()
    each = src.shape[1] * slots
    mine = pl.multiple_of(lax.axis_index("chan") * each, each)
    raw[0:each, :] = dot(hot[pl.ds(mine, each), :], latent[...]).astype(BF16)
    coefs = here[1][lax.axis_index("chan")]
    rows = [piece[x : x + 1, :] for x in range(src.shape[1]) for piece in pieces(coefs)]
    raw[each : each + VECTORS, :] = vector_rows(rows, width)


def inner_prep_kernel(neighbors, coef, _, hot, spread, neighbors_here, coef_here, sem):
    for copy in fetch_all([(neighbors, neighbors_here), (coef, coef_here)], sem):
        copy.wait()
    degree, nodes = neighbors.shape
    one_hot_rows(columns(neighbors_here[...]), columns(coef_here[...]), degree, nodes, hot, spread)


def wide(spread):
    return jnp.concatenate([spread, spread], axis=1)


def cross_sums(source, gain, hot, spread, outs):
    slots = outs[0].shape[0]
    each = hot.shape[0] // (len(outs) * slots)
    hidden = jnp.maximum(dot(hot[...], source) + wide(spread[...]) * gain, 0.0)
    for r, out in enumerate(outs):
        total = hidden[r * each * slots : (r * each + 1) * slots]
        for x in range(r * each + 1, (r + 1) * each):
            total = total + hidden[x * slots : (x + 1) * slots]
        out[...] = total.astype(BF16)


def choose(which, refs, rows):
    value = refs[0][rows, :]
    for r in range(1, len(refs)):
        value = jnp.where(which == r, refs[r][rows, :], value)
    return value


def place_of(segment, segments):
    return lax.rem(lax.axis_index("segment") - segment + segments, segments)


def edge_weights(which, j, mine, other, width):
    edge, under = edge_rows(width, j)
    a, b = (choose(which, refs, edge) for refs in (mine, other))
    first = lax.axis_index("chan") == 0
    weights = jnp.concatenate([jnp.where(first, a, b), jnp.where(first, b, a)], axis=0)
    return weights, choose(which, mine, under).astype(F32)


def partner_sums_kernel(segments, *refs):
    mine, other = refs[:segments], refs[segments : 2 * segments]
    raw, outs = refs[2 * segments : 2 * segments + 2], refs[2 * segments + 2 :]
    slots, width = outs[0].shape
    each = (raw[0].shape[0] - VECTORS) // slots
    weights, vectors = edge_weights(place_of(0, segments), 0, mine, other, width)
    for r, out in enumerate(outs):
        block = jnp.where(lax.axis_index("chan") == r, raw[0][...], raw[1][...])
        table = (dot(block[0 : each * slots, :], weights) + vectors[0:1, :]).astype(BF16).astype(F32)
        rows = block[each * slots :, 0:slots].astype(F32)
        coefs = [sum(rows[i : i + 1] for i in range(3 * x + 1, 3 * x + 3)) + rows[3 * x : 3 * x + 1] for x in range(each)]
        coefs = columns(jnp.concatenate(coefs, axis=0))
        total = None
        for x in range(each):
            hidden = table[x * slots : (x + 1) * slots] + coefs[:, x : x + 1] * vectors[1:2, :]
            hidden = jnp.maximum(hidden, 0.0)
            total = hidden if total is None else total + hidden
        out[...] = total.astype(BF16)


def inner_kernel(segments, segment, j, first, *refs):
    mine, other = refs[:segments], refs[segments : 2 * segments]
    source, hot, spread, *_, sums = refs[2 * segments :]
    nodes, width = sums.shape
    which = place_of(segment, segments)
    table = source[...]
    if first:
        weights, vectors = edge_weights(which, j, mine, other, width)
        table = (dot(table, weights) + vectors[0:1, :]).astype(BF16)
    gain = choose(which, mine, edge_rows(width, j)[1]).astype(F32)[1:2, :]
    total = None
    for k in range(hot.shape[0] // nodes):
        rows = pl.ds(k * nodes, nodes)
        hidden = jnp.maximum(dot(hot[rows, :], table) + wide(spread[rows, :]) * gain, 0.0)
        total = hidden if total is None else total + hidden
    sums[...] = total


def weights_kernel(segments, segment, j, *refs):
    mine, other, vec_mine, vec_other = (refs[i * segments : (i + 1) * segments] for i in range(4))
    latent, before, chosen = refs[4 * segments :]
    width = before.shape[1]
    half = width // 2
    inner, outer = slice(0, width), slice(width, width + half)
    which = place_of(segment, segments)
    in_a, in_b = (choose(which, refs, inner) for refs in (mine, other))
    vec_a, vec_b = (choose(which, refs, edge_rows(width, j)[1]) for refs in (vec_mine, vec_other))
    joined = jnp.concatenate([in_a[:, :half], in_b[:, :half]], axis=1)
    bias = jnp.concatenate([vec_a[:, :half], vec_b[:, :half]], axis=1).astype(F32)[4:5, :]
    before[...] = dot(latent[...], joined) + bias
    chosen[0:width, :] = jnp.concatenate([in_a[:, half:], in_b[:, half:]], axis=1)
    for start, refs in ((width, mine), (width + half, other)):
        out = choose(which, refs, outer).astype(F32)
        chosen[start : start + half, :] = (out - jnp.mean(out, axis=1, keepdims=True)).astype(BF16)
    chosen[2 * width : 2 * width + VECTORS, :] = vec_a


def node_kernel(segments, segment, j, last, rounds, *refs):
    arrived, refs = refs[:rounds], refs[rounds:]
    latent, sums, before, chosen, scatter = refs[:5]
    width = sums.shape[1]
    half = width // 2
    nodes = sums.shape[0]
    mine, other = refs[5 : 5 + segments], refs[5 + segments : 5 + 2 * segments]
    if last:
        (result,) = refs[5:]
    else:
        hot, spread, result, source, *outs = refs[5 + 2 * segments :]
        weights, edge_vectors = edge_weights(
            place_of(segment, segments), j, mine, other, width
        )
    blocks = jnp.concatenate([block[...] for block in arrived[::-1]], axis=0)
    vectors = chosen[2 * width : 2 * width + VECTORS, :].astype(F32)
    summed = sums[...] + dot(scatter[...], blocks)
    hidden = before[...] + dot(summed.astype(BF16), chosen[0:width, :])
    hidden = jnp.maximum(hidden, 0.0).astype(BF16)
    centred = dot(hidden, chosen[width : 2 * width, :])
    variance = jnp.mean(centred * centred, axis=1, keepdims=True)
    normed = centred * lax.rsqrt(variance + 1e-05) * vectors[2:3, :] + vectors[3:4, :]
    fresh = (latent[...].astype(F32) + normed).astype(BF16)
    if last:
        result[0] = fresh
        return
    result[...] = fresh
    table = (dot(fresh, weights) + edge_vectors[0:1, :]).astype(BF16)
    source[...] = table
    cross_sums(table, edge_vectors[1:2, :], hot, spread, outs)


def partner_route(count, r):
    return [(i, i ^ 1 << r) for i in range(count) if i ^ 1 << r < count]


def per_device(
    latents,
    neighbors,
    edge_coef,
    cross_src,
    cross_coef,
    recv_node,
    w_edge,
    w_node_in,
    w_node_out,
    edge_bias,
    edge_gain,
    node_bias,
    norm_gain,
    norm_bias,
):
    segments, cores, parts = (lax.axis_size(a) for a in ("segment", "chan", "dom"))
    micro, nodes, width = latents.shape
    held = w_edge.shape[0]
    rounds, slots = recv_node.shape
    degree, edges = neighbors.shape[0], cross_src.shape[0] * cross_src.shape[1]
    half = width // 2
    assert micro == segments and cores == rounds == 2

    def in_hbm(*arrays):
        return [pltpu.with_memory_space_constraint(array, pltpu.HBM) for array in arrays]

    def buffers(*arrays):
        return [pltpu.VMEM(array.shape, array.dtype) for array in arrays]

    def swap(block):
        return lax.ppermute(block, "chan", [(0, 1), (1, 0)])

    def exchange(blocks):
        return [lax.ppermute(block, "dom", partner_route(parts, r)) for r, block in enumerate(blocks)]

    def once(arrays, made):
        return lax.optimization_barrier((arrays, made))[0]

    vectors = (edge_bias, edge_gain, norm_gain, norm_bias, node_bias)
    edge_pack, *node_packs = kernel_call(
        pack_kernel,
        [shape((edge_rows(width, held)[0].start, width), BF16)] + [shape((width + half, width), BF16)] * held,
        [*in_hbm(w_edge, w_node_in, w_node_out, *vectors)],
        1 << 33,
        scratch=[*buffers(*vectors), pltpu.SemaphoreType.DMA((5 + 4 * held,))],
    )
    graph = (cross_src, cross_coef, recv_node)
    latent, hot_c, spread_c, scatter, raw = kernel_call(
        cross_prep_kernel,
        [
            shape((nodes, width), BF16),
            shape((edges * slots, nodes), BF16),
            shape((edges * slots, LANES), F32),
            shape((nodes, rounds * slots), BF16),
            shape((edges // rounds * slots + VECTORS, width), BF16),
        ],
        [*in_hbm(latents, *graph), edge_pack],
        1 << 28,
        after=1,
        scratch=[*buffers(*graph), pltpu.SemaphoreType.DMA((4,))],
    )
    route = []
    for core in range(cores):
        route += [(a * cores + core, b * cores + core) for a, b in partner_route(parts, core)]
    raw = lax.ppermute(raw, ("dom", "chan"), route)
    hot, spread = kernel_call(
        inner_prep_kernel,
        [shape((degree * nodes, nodes), BF16), shape((degree * nodes, LANES), F32)],
        [*in_hbm(neighbors, edge_coef), scatter],
        1 << 30,
        after=1,
        scratch=[*buffers(neighbors, edge_coef), pltpu.SemaphoreType.DMA((2,))],
    )
    routes = [[(i, (i + r) % segments) for i in range(segments)] for r in range(1, segments)]

    def spread_out(pack):
        return [lax.ppermute(pack, "segment", route) for route in routes]

    edges_mine = spread_out(edge_pack)
    nodes_mine = [spread_out(once(pack, scatter) if j else pack) for j, pack in enumerate(node_packs)]

    def swaps(own, received, made):
        return [own, *received, swap(once(own, scatter)), *map(swap, once(received, made))]

    def crossed(pack):
        return [
            lax.ppermute(
                pack,
                ("segment", "chan"),
                [(a * cores + core, b * cores + 1 - core) for a, b in route for core in range(cores)],
            )
            for route in routes
        ]

    weights = swaps(edge_pack, edges_mine, (raw, hot))
    node_weights = [None] * held
    node_weights[0] = swaps(node_packs[0], nodes_mine[0], weights[-1])
    for j in range(1, held):
        pack = once(node_packs[j], scatter)
        node_weights[j] = [node_packs[j], *nodes_mine[j], swap(once(node_packs[j], scatter)), *crossed(pack)]
    total = segments * held
    sends = [shape((nodes, width), BF16)] + [shape((slots, width), BF16)] * rounds
    source = latent
    for layer in range(total):
        segment, j = divmod(layer, held)
        sums = kernel_call(
            functools.partial(inner_kernel, segments, segment, j, layer == 0),
            shape((nodes, width), F32),
            [*weights, source, hot, spread, *(() if layer else [raw, *nodes_mine[0]])],
            1 << 31 if layer == 0 else 1 << 31,
            after=0 if layer else len([raw, *nodes_mine[0]]),
        )
        if layer == 0:
            arrived = kernel_call(
                functools.partial(partner_sums_kernel, segments),
                sends[1:],
                [*weights, raw, swap(raw)],
                1 << 28,
            )
        else:
            arrived = exchange(blocks)
        before, chosen = kernel_call(
            functools.partial(weights_kernel, segments, segment, j),
            [shape((nodes, width), F32), shape((2 * width + VECTORS, width), BF16)],
            [*node_weights[j], *weights, latent],
            1 << 28,
        )
        operands = [*arrived[::-1], latent, sums, before, chosen, scatter]
        last = layer == total - 1
        follow, step = divmod(layer + 1, held)
        if last:
            outs = [shape((1, nodes, width), BF16)]
        else:
            operands += [*weights, hot_c, spread_c]
            outs = [shape((nodes, width), BF16), *sends]
        latent, *rest = kernel_call(
            functools.partial(node_kernel, segments, follow, step, last, rounds), outs, operands, 1 << 30 if layer == 0 else 1 << 30
        )
        if not last:
            source, *blocks = rest
    return latent


def solution(mesh):
    return jax.shard_map(
        per_device,
        mesh=mesh,
        in_specs=(
            P(None, ("groups", "dom"), None),
            P(None, ("groups", "dom")),
            P(None, ("groups", "dom")),
            P(None, None, ("groups", "dom")),
            P(None, None, ("groups", "dom")),
            P(None, ("groups", "dom")),
            P("segment", None, None),
            P("segment", None, "chan"),
            P("segment", "chan", None),
            P("segment", None),
            P("segment", None),
            P("segment", "chan"),
            P("segment", None),
            P("segment", None),
        ),
        out_specs=P("segment", ("groups", "dom"), None),
        check_vma=False,
    )
```
